128 devices in a mesh: dp: 8 (over z_hi, y), tensor: 16 (over x, z_lo, core).
Axes of the slice: x: 4, y: 4, z: 4 (z_hi: 2, z_lo: 2; z = z_hi * 2 + z_lo), core: 2. Of those that a mesh axis runs over, the one named last changes fastest.
Arguments:
- hidden: bfloat16 [4096, 53248], P('dp', 'tensor'), may hold values from -6 to 6
- cotangent: bfloat16 [4096, 16384], P('dp', 'tensor'), may hold values from -96 to 96
- prompt_group_index: int32 [4096], P('dp'), may hold values from 0 to 511
- answer_token_mask: int32 [4096], P('dp'), may hold values 0 or 1
- token_reward_order: int32 [4096], P('dp'), may hold values from 0 to 15
- source_lowdim_matrix: float32 [32, 53248], P(None, 'tensor'), may hold values from -0.02734375 to 0.02734375
- running_mean_source_matrix: float32 [32, 53248], P(None, 'tensor'), may hold values from -6 to 6
- running_variance_source_matrix: float32 [32, 53248], P(None, 'tensor'), may hold values from 0.01 to 1
- target_lowdim_matrix: float32 [32, 16384], P(None, 'tensor'), may hold values from -1 to 1
- running_mean_target_matrix: float32 [32, 16384], P(None, 'tensor'), may hold values from -0.6 to 0.6
- running_variance_target_matrix: float32 [32, 16384], P(None, 'tensor'), may hold values from 0.0001 to 0.01
- frozen_down_weight: bfloat16 [53248, 16384], P('tensor', 'dp'), may hold values from -0.02734375 to 0.02734375
- sampled_token_input: bfloat16 [512, 53248], P(None, 'tensor'), may hold values from -6 to 6
Outputs:
- rollout_out: bfloat16 [512, 16384], P(None, ('dp', 'tensor'))
- next_left_factor: float32 [32, 53248], P('dp', 'tensor')
- next_first_moment_left: float32 [32, 53248], P('dp', 'tensor')
- next_second_moment_left: float32 [32, 53248], P('dp', 'tensor')
- next_right_factor: float32 [32, 16384], P('dp', 'tensor')
- next_first_moment_right: float32 [32, 16384], P('dp', 'tensor')
- next_second_moment_right: float32 [32, 16384], P('dp', 'tensor')
The draws below stay inside these ranges and needn't reach their ends.
All inputs are finite; a program needn't handle non-finite values. No bound on the sum of `answer_token_mask` on one device may be relied on, other than what follows from the above.
Results may differ from the reference program's by a relative error of at most 0.0063.
Values may be sent and summed in bfloat16 or wider, within the bound.
A program may use at most 128 MiB of HBM per device.

```python
import math
import jax
import jax.numpy as jnp
from jax import lax

EMBEDDING_SIZE = 16384
INNER_NEURONS = 53248
LATENT_DIMENSION = 32
ROLLOUT = 512
TOKENS = 4096
GROUPS = 512
N_TENSOR = 16


def with_ends(entries, stream_key, smallest, high):
    index_at = [jax.random.randint(jax.random.fold_in(stream_key, axis), (), 0, length) for axis, length in enumerate(entries.shape)]
    main_axis = entries.shape.index(max(entries.shape))
    next_to = index_at[:main_axis] + [(index_at[main_axis] + 1) % entries.shape[main_axis]] + index_at[main_axis + 1:]
    return entries.at[tuple(index_at)].set(smallest).at[tuple(next_to)].set(high)


def level_of(key, shape, split, low, largest):
    level, own = 1.0, jax.random.fold_in(key, 6)
    for axis_at, blocks in split:
        steps = jnp.exp(jax.random.uniform(jax.random.fold_in(own, axis_at), (blocks,), jnp.float32, low / len(split), largest / len(split)))
        level = level * jnp.repeat(steps, shape[axis_at] // blocks).reshape([-1 if axis == axis_at else 1 for axis in range(len(shape))])
    return level


def gaussian(own_key, extent, deviation, bound, shards=(), kind=jnp.bfloat16):
    entries = deviation * jax.random.normal(own_key, extent, jnp.float32)
    if shards:
        entries = entries * level_of(own_key, extent, shards, -0.22, 0.18)
    return jnp.clip(entries, -bound, bound).astype(kind)


def setup_inputs(seed: int = 0) -> dict:
    streams_of = jax.random.split(jax.random.key(seed), 14)
    return {
        "hidden": gaussian(streams_of[0], (TOKENS, INNER_NEURONS), 1.0, 6.0, ((0, 8), (1, 16))),
        "cotangent": gaussian(streams_of[1], (TOKENS, EMBEDDING_SIZE), 16.0, 96.0, ((0, 8), (1, 16))),
        "prompt_group_index": with_ends(jax.random.randint(streams_of[2], (TOKENS,), 0, GROUPS), jax.random.fold_in(streams_of[2], 1), 0, GROUPS - 1).astype(jnp.int32),
        "answer_token_mask": with_ends((jax.random.randint(streams_of[3], (TOKENS,), 0, 4) < 3).astype(jnp.int32), jax.random.fold_in(streams_of[3], 1), 0, 1),
        "token_reward_order": with_ends(jax.random.randint(streams_of[4], (TOKENS,), 0, 16), jax.random.fold_in(streams_of[4], 1), 0, 15).astype(jnp.int32),
        "source_lowdim_matrix": gaussian(streams_of[5], (LATENT_DIMENSION, INNER_NEURONS), INNER_NEURONS ** -0.5, 0.02734375, ((1, 16),), jnp.float32),
        "running_mean_source_matrix": gaussian(streams_of[6], (LATENT_DIMENSION, INNER_NEURONS), 1.0, 6.0, ((1, 16),), jnp.float32),
        "running_variance_source_matrix": jnp.clip(jnp.exp(math.log(1.0) - 4.6051702 * jax.random.uniform(streams_of[7], (LATENT_DIMENSION, INNER_NEURONS), jnp.float32) ** level_of(streams_of[7], (LATENT_DIMENSION, INNER_NEURONS), ((1, 16),), -0.2, 0.2)), 0.01, 1.0),
        "target_lowdim_matrix": gaussian(streams_of[8], (LATENT_DIMENSION, EMBEDDING_SIZE), LATENT_DIMENSION ** -0.5, 1.0, ((1, 16),), jnp.float32),
        "running_mean_target_matrix": gaussian(streams_of[9], (LATENT_DIMENSION, EMBEDDING_SIZE), 0.1, 0.6, ((1, 16),), jnp.float32),
        "running_variance_target_matrix": jnp.clip(jnp.exp(math.log(0.01) - 4.6051702 * jax.random.uniform(streams_of[10], (LATENT_DIMENSION, EMBEDDING_SIZE), jnp.float32) ** level_of(streams_of[10], (LATENT_DIMENSION, EMBEDDING_SIZE), ((1, 16),), -0.2, 0.2)), 0.0001, 0.01),
        "frozen_down_weight": gaussian(streams_of[11], (INNER_NEURONS, EMBEDDING_SIZE), INNER_NEURONS ** -0.5, 0.02734375, ((0, 16), (1, 8))),
        "sampled_token_input": gaussian(streams_of[12], (ROLLOUT, INNER_NEURONS), 1.0, 6.0, ((1, 16),)),
    }


adapter_scale = 2.0
bias_one = 1.0 - 0.9 ** 10
bias_two = 1.0 - 0.999 ** 10

def adaptive_moment_step(param, grad, first, second):
    first = 0.9 * first + 0.1 * grad
    second = 0.999 * second + 0.001 * grad * grad
    param = param - 0.004 * (first / bias_one) / (jnp.sqrt(second / bias_two) + 1e-08)
    return (param, first, second)

def reference(hidden, cotangent, prompt_group_index, answer_token_mask, token_reward_order, source_lowdim_matrix, running_mean_source_matrix, running_variance_source_matrix, target_lowdim_matrix, running_mean_target_matrix, running_variance_target_matrix, frozen_down_weight, sampled_token_input):
    left_factor_value = source_lowdim_matrix.astype(jnp.bfloat16)
    rank_projection = jnp.dot(hidden, left_factor_value.T, preferred_element_type=jnp.float32)
    mask_float = answer_token_mask.astype(jnp.float32)
    rank_float = token_reward_order.astype(jnp.float32)
    member = (prompt_group_index[:, None] == jnp.arange(GROUPS, dtype=jnp.int32)[None, :]).astype(jnp.float32)
    masked = member * mask_float[:, None]
    counts = lax.optimization_barrier(jnp.sum(masked, axis=0))
    sums = lax.optimization_barrier(jnp.sum(masked * rank_float[:, None], axis=0))
    squares = lax.optimization_barrier(jnp.sum(masked * (rank_float * rank_float)[:, None], axis=0))
    safe_counts = jnp.maximum(counts, 1.0)
    mean = sums / safe_counts
    spread = jnp.maximum(jnp.sqrt(jnp.maximum(squares / safe_counts - mean * mean, 0.0)), 1.0)
    total = jnp.maximum(jnp.sum(counts), 1.0)
    coefficient = -mask_float * (rank_float - mean[prompt_group_index]) / spread[prompt_group_index] / total
    incoming_gradient = coefficient[:, None] * cotangent.astype(jnp.float32)
    backward_gradient = jnp.dot(incoming_gradient, target_lowdim_matrix.T, precision=lax.Precision.HIGHEST).astype(jnp.bfloat16)
    left_factor_gradient = adapter_scale * jnp.dot(backward_gradient.T, hidden, preferred_element_type=jnp.float32)
    right_factor_gradient = adapter_scale * jnp.dot(rank_projection.T, incoming_gradient, precision=lax.Precision.HIGHEST)
    next_left_factor, next_first_moment_left, next_second_moment_left = adaptive_moment_step(source_lowdim_matrix, left_factor_gradient, running_mean_source_matrix, running_variance_source_matrix)
    next_right_factor, next_first_moment_right, next_second_moment_right = adaptive_moment_step(target_lowdim_matrix, right_factor_gradient, running_mean_target_matrix, running_variance_target_matrix)
    a_send = next_left_factor.astype(jnp.bfloat16)
    b_send = next_right_factor.astype(jnp.bfloat16)
    rows = INNER_NEURONS // N_TENSOR

    def merge_step(total_out, index):
        start = (index * rows).astype(jnp.int32)
        frozen_weight_block = lax.dynamic_slice_in_dim(frozen_down_weight, start, rows, 0)
        a_block = lax.dynamic_slice_in_dim(a_send, start, rows, 1)
        x_block = lax.dynamic_slice_in_dim(sampled_token_input, start, rows, 1)
        adapter_product = jnp.dot(a_block.T, b_send, preferred_element_type=jnp.float32)
        combined_weight = (frozen_weight_block.astype(jnp.float32) + adapter_scale * adapter_product).astype(jnp.bfloat16)
        return (total_out + jnp.dot(x_block, combined_weight, preferred_element_type=jnp.float32), None)
    start_total = jnp.zeros((sampled_token_input.shape[0], frozen_down_weight.shape[1]), jnp.float32)
    summed, _ = lax.scan(merge_step, start_total, jnp.arange(N_TENSOR, dtype=jnp.int32))
    rollout_out = summed.astype(jnp.bfloat16)
    return (rollout_out, next_left_factor, next_first_moment_left, next_second_moment_left, next_right_factor, next_first_moment_right, next_second_moment_right)
```

```python
import functools

import jax
import jax.numpy as jnp
from jax import lax
from jax.experimental import pallas as pl
from jax.experimental.pallas import tpu as pltpu
from jax.sharding import PartitionSpec as P

MESH = pl.DeviceIdType.MESH
F32 = jnp.float32
BF16 = jnp.bfloat16

adapter_scale = 2.0
bias_one = 1.0 - 0.9**10
bias_two = 1.0 - 0.999**10

GAP_ONE, GAP_TWO = 2, 4


def contract(left, right, left_dim, right_dim):
    return lax.dot_general(
        left, right, (((left_dim,), (right_dim,)), ((), ())), preferred_element_type=F32
    )


def high_low(value):
    high = value.astype(BF16)
    return high, (value - high.astype(F32)).astype(BF16)


def quarters(value, width):
    return jnp.concatenate([value[:, q * width : (q + 1) * width] for q in range(4)], axis=0)


def kernel(
    nd, nt,
    hidden, cotangent, groups, mask, order, a_in, ma_in, va_in, b_in, mb_in, vb_in, weight, sampled,
    out, pa_out, ma_out, va_out, pb_out, mb_out, vb_out,
    hid, cot, grp, msk, odr, a, ma, va, b, mb, vb, w, x,
    stat, stat_r, coef, s1, r1, full, g, gf, gs, gr, own, xa_s, xa_r, xall, bs, bd,
    keep, give, got, big, big_r,
    o_out, o_pa, o_ma, o_va, o_pb, o_mb, o_vb,
    lsem, wsem, osem, pair_sem, got_sem, big_sem, big_rsem, bs_sem, chain_sem,
):
    i = lax.axis_index("dp")
    t = lax.axis_index("tensor")
    core = lax.rem(t, 2)
    chip = t // 2
    chips = nt // 2
    half_rows = chip * 8
    inner = hid.shape[1]
    width = cot.shape[1]
    quarter = gs.shape[2]
    n_tok = hid.shape[0]
    half_tok = n_tok // 2

    b_home = t // 8
    own_b = jnp.logical_and(t // 2 == i, t - 8 * core >= 0)
    own_b = jnp.logical_and(own_b, t - 8 * core < 8)
    b_source = 2 * i + b_home
    barrier = pltpu.get_barrier_semaphore()

    def greet_tensor(d, _):
        pl.semaphore_signal(
            barrier, inc=1, device_id={"tensor": lax.rem(t + d, nt)}, device_id_type=MESH
        )
        return _

    def greet_dp(d, _):
        pl.semaphore_signal(
            barrier, inc=1, device_id={"dp": lax.rem(i + d, nd)}, device_id_type=MESH
        )
        return _

    def greet_source(r, carry):
        @pl.when(jnp.logical_or(r != i, b_source != t))
        def _():
            pl.semaphore_signal(
                barrier, inc=1, device_id={"dp": r, "tensor": b_source}, device_id_type=MESH
            )

        return carry

    loads = [
        (groups, grp), (mask, msk), (order, odr), (a_in, a), (b_in, b), (cotangent, cot),
    ]
    load = [pltpu.make_async_copy(src, dst, lsem.at[n]) for n, (src, dst) in enumerate(loads)]
    for copy in load:
        copy.start()
    pieces = 2
    piece = inner // pieces
    hid_load = []
    for n in range(pieces):
        cols = pl.ds(n * piece, piece)
        hid_load.append(
            pltpu.make_async_copy(hidden.at[:, cols], hid.at[:, cols], lsem.at[6 + n])
        )
        hid_load[-1].start()

    lax.fori_loop(1, nt, greet_tensor, 0)
    lax.fori_loop(1, nd, greet_dp, 0)
    lax.fori_loop(0, nd, greet_source, 0)

    x_load = pltpu.make_async_copy(sampled, x, lsem.at[8])

    def block_of(s):
        return lax.rem(chip + 1 + s, chips)

    def w_load(s):
        cols = pl.ds(pl.multiple_of(block_of(s) * 256, 256), 256)
        return pltpu.make_async_copy(weight.at[:, cols], w.at[s], wsem.at[s])

    late = [
        pltpu.make_async_copy(src, dst, lsem.at[9 + n])
        for n, (src, dst) in enumerate([(ma_in, ma), (va_in, va), (mb_in, mb), (vb_in, vb)])
    ]

    for n in range(3):
        load[n].wait()
    mask_row = msk[...].astype(F32)
    rank_row = odr[...].astype(F32)
    n_groups = stat.shape[1]
    group_id = lax.broadcasted_iota(jnp.int32, (n_groups, n_tok), 0)
    member = jnp.where(group_id == grp[...], 1.0, 0.0).astype(BF16)
    row = lax.broadcasted_iota(jnp.int32, (8, n_tok), 0)
    weighted = mask_row * rank_row
    terms = jnp.where(
        row == 0, mask_row, jnp.where(row == 1, weighted, jnp.where(row == 2, weighted * rank_row, 0.0))
    )
    stat[...] = contract(terms.astype(BF16), member, 1, 1)

    load[4].wait()
    load[5].wait()
    b_high, b_low = high_low(b[...])
    raw = contract(jnp.concatenate([b_high, b_low], axis=0), cot[...], 1, 1)
    s1[32:64, :] = raw[0:32] + raw[32:64]

    pl.semaphore_wait(barrier, (nt - 1) + (nd - 1) + 8 - own_b.astype(jnp.int32))

    def to_dp(src, dst, sems):
        def body(d, _):
            pltpu.make_async_remote_copy(
                src_ref=src(lax.rem(i + d, nd)), dst_ref=dst(d),
                send_sem=chain_sem.at[sems], recv_sem=chain_sem.at[sems + 1],
                device_id={"dp": lax.rem(i + d, nd)}, device_id_type=MESH,
            ).start()
            return _

        lax.fori_loop(1, nd, body, 0)

    def to_tensor(src, dst, sems):
        def body(d, _):
            pltpu.make_async_remote_copy(
                src_ref=src(lax.rem(t + d, nt)), dst_ref=dst(d),
                send_sem=chain_sem.at[sems], recv_sem=chain_sem.at[sems + 1],
                device_id={"tensor": lax.rem(t + d, nt)}, device_id_type=MESH,
            ).start()
            return _

        lax.fori_loop(1, nt, body, 0)

    def arrived(ref, sems):
        pltpu.make_async_copy(ref, ref, chain_sem.at[sems + 1]).wait()

    def sent(ref, sems):
        pltpu.make_async_copy(ref, ref, chain_sem.at[sems]).wait()

    to_dp(lambda r: stat, lambda d: stat_r.at[d - 1], 0)

    load[3].wait()
    a_half = a[...].astype(BF16)
    total = None
    for n in range(pieces):
        hid_load[n].wait()
        if n == 0:
            x_load.start()
            for s in range(2):
                w_load(s).start()
        cols = slice(n * piece, (n + 1) * piece)
        part = contract(a_half[:, cols], hid[:, cols], 1, 1)
        total = part if total is None else total + part
    for s in range(2, chips):
        w_load(s).start()
    for copy in late:
        copy.start()
    s1[0:32, :] = total

    def chunk(ref, k):
        rows = pl.ds(pl.multiple_of((k // 2) * 8, 8), 8)
        cols = pl.ds(pl.multiple_of(lax.rem(k, 2) * half_tok, half_tok), half_tok)
        return ref.at[rows, cols]

    to_tensor(lambda k: chunk(s1, k), lambda d: r1.at[d - 1], 2)

    def partner(t):
        return t + 1 - 2 * core

    def pair_copy(s):
        return pltpu.make_async_remote_copy(
            src_ref=give.at[s], dst_ref=got.at[s], send_sem=pair_sem.at[s], recv_sem=got_sem.at[s],
            device_id={"tensor": partner(t)}, device_id_type=MESH,
        )

    def compute(s, _):
        w_load(s).wait()
        block = contract(x[...], w[s], 1, 0)
        first, second = block[:, :128], block[:, 128:]
        keep[s] = jnp.where(core == 0, first, second)
        give[s] = jnp.where(core == 0, second, first).astype(BF16)
        pair_copy(s).start()
        return _

    def big_copy(s):
        return pltpu.make_async_remote_copy(
            src_ref=big.at[s], dst_ref=big_r.at[s], send_sem=big_sem.at[s], recv_sem=big_rsem.at[s],
            device_id={"tensor": 2 * block_of(s) + core}, device_id_type=MESH,
        )

    def forward(s, _):
        pair_copy(s).wait_recv()
        big[s] = (keep[s] + got[s].astype(F32)).astype(BF16)
        big_copy(s).start()
        return _

    x_load.wait()
    lax.fori_loop(0, GAP_ONE, compute, 0)

    arrived(stat_r, 0)
    stats = stat[...]
    for d in range(nd - 1):
        stats = stats + stat_r[d]
    counts, sums, squares = stats[0:1], stats[1:2], stats[2:3]
    safe = jnp.maximum(counts, 1.0)
    mean = sums / safe
    spread = jnp.maximum(jnp.sqrt(jnp.maximum(squares / safe - mean * mean, 0.0)), 1.0)
    every = jnp.maximum(jnp.sum(counts, axis=1, keepdims=True), 1.0)
    table = jnp.zeros((8, n_groups), F32)
    row_g = lax.broadcasted_iota(jnp.int32, (8, n_groups), 0)
    for base, value in ((0, mean), (3, spread)):
        rest = value
        for n in range(3):
            term = rest.astype(BF16).astype(F32)
            table = jnp.where(row_g == base + n, term, table)
            rest = rest - term
    looked = contract(table.astype(BF16), member, 1, 0)
    mean_t = (looked[0:1] + looked[1:2]) + looked[2:3]
    spread_t = (looked[3:4] + looked[4:5]) + looked[5:6]
    coef[...] = jnp.broadcast_to(-mask_row * (rank_row - mean_t) / spread_t / every, (8, n_tok))

    arrived(r1, 2)
    mine = chunk(s1, t)[...]
    for d in range(nt - 1):
        mine = mine + r1[d]
    half = pl.ds(pl.multiple_of(core * half_tok, half_tok), half_tok)
    full_mine = chunk(full, t)
    full_mine[...] = mine * coef[:, half]
    to_tensor(lambda k: chunk(full, t), lambda d: chunk(full, t), 4)

    lax.fori_loop(GAP_ONE, GAP_TWO, compute, 0)

    for copy in late:
        copy.wait()

    def own_rows(value_a, value_b, slot):
        rows = pl.ds(pl.multiple_of((i // 2) * 8, 8), 8)
        odd = lax.rem(i, 2) == 1

        def pick(ref):
            eight = ref[rows, :]
            return jnp.where(odd, eight[4:8], eight[0:4])

        pad = jnp.zeros((4, 4 * quarter - inner - width), F32)
        own[slot] = quarters(jnp.concatenate([pick(value_a), pick(value_b), pad], axis=1), quarter)

    own_rows(a, b, 0)
    own_rows(ma, mb, 1)
    own_rows(va, vb, 2)

    arrived(r1, 4)
    back = full[32:64, :].astype(BF16)
    p_high, p_low = high_low(full[0:32, :])
    g[:, 0:inner] = adapter_scale * contract(back, hid[...], 1, 0)
    right = contract(jnp.concatenate([p_high, p_low], axis=0), cot[...], 1, 0)
    g[:, inner : inner + width] = adapter_scale * (right[0:32] + right[32:64])
    g[:, inner + width :] = jnp.zeros((32, 4 * quarter - inner - width), F32)
    for r in range(nd):
        value = quarters(g[4 * r : 4 * r + 4, :], quarter)
        gf[r] = value
        gs[r] = value.astype(BF16)
    to_dp(lambda r: gs.at[r], lambda d: gr.at[d - 1], 6)

    lax.fori_loop(0, GAP_ONE, forward, 0)

    def both(s, _):
        compute(s, 0)
        forward(s - (GAP_TWO - GAP_ONE), 0)
        return _

    lax.fori_loop(GAP_TWO, chips, both, 0)

    arrived(gr, 6)
    grad = gf[i]
    for d in range(nd - 1):
        grad = grad + gr[d].astype(F32)
    first = 0.9 * own[1] + 0.1 * grad
    second = 0.999 * own[2] + 0.001 * grad * grad
    param = own[0] - 0.004 * (first / bias_one) / (jnp.sqrt(second / bias_two) + 1e-08)
    a_send = param.astype(BF16)
    rounded = a_send.astype(F32)
    for k in range(8):
        at = inner + 128 * k
        q, c = at // quarter, at % quarter
        part = rounded[4 * q : 4 * q + 4, c : c + 128]
        bs[k] = jnp.concatenate([part, part], axis=0)

    def b_copy(k):
        return pltpu.make_async_remote_copy(
            src_ref=bs.at[k], dst_ref=bd.at[i], send_sem=bs_sem.at[k], recv_sem=chain_sem.at[12],
            device_id={"dp": t // 2, "tensor": 8 * core + k}, device_id_type=MESH,
        )

    def b_here(k):
        return jnp.logical_and(t // 2 == i, 8 * core + k == t)

    def send_b(k, carry):
        @pl.when(jnp.logical_not(b_here(k)))
        def _():
            b_copy(k).start()

        @pl.when(b_here(k))
        def _():
            pltpu.make_async_copy(bs.at[k], bd.at[i], chain_sem.at[12]).start()

        return carry

    partial = None
    for q in range(4):
        cols = min(quarter, inner - q * quarter)
        if cols <= 0:
            continue
        part = contract(a_send[:, :cols], x[:, q * quarter : q * quarter + cols], 1, 1)
        part = part[4 * q : 4 * q + 4]
        partial = part if partial is None else partial + part
    xa_s[...] = jnp.concatenate([partial[:, :half_tok], partial[:, half_tok:]], axis=0)
    to_tensor(lambda k: xa_s, lambda d: xa_r.at[d - 1], 8)
    lax.fori_loop(0, 8, send_b, 0)

    def split(value, left_ref, right_ref):
        for q in range(4):
            lo, hi = q * quarter, (q + 1) * quarter
            rows = value[4 * q : 4 * q + 4]
            if lo < inner:
                left_ref[:, lo : min(hi, inner)] = rows[:, : min(hi, inner) - lo]
            start, stop = max(lo, inner), min(hi, inner + width)
            if start < stop:
                right_ref[:, start - inner : stop - inner] = rows[:, start - lo : stop - lo]

    split(param, o_pa, o_pb)
    split(first, o_ma, o_mb)
    split(second, o_va, o_vb)
    outs = [
        (o_pa, pa_out), (o_ma, ma_out), (o_va, va_out), (o_pb, pb_out), (o_mb, mb_out), (o_vb, vb_out),
    ]
    stores = [pltpu.make_async_copy(src, dst, osem.at[n]) for n, (src, dst) in enumerate(outs)]
    for copy in stores:
        copy.start()

    lax.fori_loop(chips - (GAP_TWO - GAP_ONE), chips - 1, forward, 0)

    arrived(xa_r, 8)
    mine = xa_s[...]
    for d in range(nt - 1):
        mine = mine + xa_r[d]
    xall[i] = mine
    to_dp(lambda r: xall.at[i], lambda d: xall.at[i], 10)

    pair_copy(chips - 1).wait_recv()
    keep[chips - 1] = keep[chips - 1] + got[chips - 1].astype(F32)
    for s in range(chips - 1):
        big_copy(s).wait_recv()
    summed = keep[chips - 1]
    for s in range(chips - 1):
        summed = summed + big_r[s].astype(F32)
    keep[chips - 1] = summed

    pltpu.make_async_copy(bd, bd, chain_sem.at[12]).wait()
    pltpu.make_async_copy(xa_r.at[pl.ds(0, nd - 1)], xa_r.at[pl.ds(0, nd - 1)], chain_sem.at[11]).wait()
    z_high, z_low = high_low(xall[...].reshape(8 * nd, half_tok))
    z = jnp.concatenate([z_high, z_low], axis=0)
    b_rows = bd[...].reshape(8 * nd, 128)
    row_b = lax.rem(lax.broadcasted_iota(jnp.int32, (8 * nd, 128), 0), 8)
    for h in range(2):
        b_half = jnp.where((row_b < 4) == (h == 0), b_rows, 0.0).astype(BF16)
        added = contract(z, jnp.concatenate([b_half, b_half], axis=0), 0, 0)
        rows = slice(h * half_tok, (h + 1) * half_tok)
        o_out[rows, :] = (keep[chips - 1, rows, :] + adapter_scale * added).astype(BF16)
    last = pltpu.make_async_copy(o_out, out, osem.at[6])
    last.start()

    sent(stat_r, 0)
    sent(r1, 2)
    sent(r1, 4)
    sent(gr, 6)
    sent(xa_r, 8)
    sent(xa_r.at[pl.ds(0, nd - 1)], 10)
    for s in range(chips):
        pair_copy(s).wait_send()
    for s in range(chips - 1):
        big_copy(s).wait_send()

    def b_sent(k, carry):
        @pl.when(jnp.logical_not(b_here(k)))
        def _():
            b_copy(k).wait_send()

        return carry

    lax.fori_loop(0, 8, b_sent, 0)
    for copy in stores:
        copy.wait()
    last.wait()


def shards(
    hidden, cotangent, prompt_group_index, answer_token_mask, token_reward_order,
    source_lowdim_matrix, running_mean_source_matrix, running_variance_source_matrix,
    target_lowdim_matrix, running_mean_target_matrix, running_variance_target_matrix,
    frozen_down_weight, sampled_token_input,
):
    nd, nt = lax.axis_size("dp"), lax.axis_size("tensor")
    tokens, inner = hidden.shape
    width = cotangent.shape[1]
    rank = source_lowdim_matrix.shape[0]
    columns = frozen_down_weight.shape[1]
    rollout = sampled_token_input.shape[0]
    n_groups = tokens * nd // 8
    chips = nt // 2
    quarter = -(-(inner + width) // 512) * 128
    rows = rank // nd
    vmem, dma = pltpu.VMEM, pltpu.SemaphoreType.DMA
    i32 = jnp.int32
    scratch = [
        vmem((tokens, inner), BF16), vmem((tokens, width), BF16),
        vmem((1, tokens), i32), vmem((1, tokens), i32), vmem((1, tokens), i32),
        vmem((rank, inner), F32), vmem((rank, inner), F32), vmem((rank, inner), F32),
        vmem((rank, width), F32), vmem((rank, width), F32), vmem((rank, width), F32),
        vmem((chips, inner, 256), BF16), vmem((rollout, inner), BF16),
        vmem((8, n_groups), F32), vmem((nd - 1, 8, n_groups), F32), vmem((8, tokens), F32),
        vmem((64, tokens), F32), vmem((nt - 1, 8, tokens // 2), F32), vmem((64, tokens), F32),
        vmem((rank, 4 * quarter), F32), vmem((nd, 16, quarter), F32), vmem((nd, 16, quarter), BF16),
        vmem((nd - 1, 16, quarter), BF16), vmem((3, 16, quarter), F32),
        vmem((8, rollout // 2), F32), vmem((nt - 1, 8, rollout // 2), F32),
        vmem((nd, 8, rollout // 2), F32), vmem((8, 8, 128), F32), vmem((nd, 8, 128), F32),
        vmem((chips, rollout, 128), F32), vmem((chips, rollout, 128), BF16),
        vmem((chips, rollout, 128), BF16), vmem((chips - 1, rollout, 128), BF16),
        vmem((chips - 1, rollout, 128), BF16),
        vmem((rollout, 128), BF16),
        vmem((rows, inner), F32), vmem((rows, inner), F32), vmem((rows, inner), F32),
        vmem((rows, width), F32), vmem((rows, width), F32), vmem((rows, width), F32),
        dma((13,)), dma((chips,)), dma((7,)), dma((chips,)), dma((chips,)),
        dma((chips - 1,)), dma((chips - 1,)), dma((8,)), dma((13,)),
    ]
    left = jax.ShapeDtypeStruct((rows, inner), F32)
    right = jax.ShapeDtypeStruct((rows, width), F32)
    return pl.pallas_call(
        functools.partial(kernel, nd, nt),
        out_shape=(jax.ShapeDtypeStruct((rollout, 128), BF16), left, left, left, right, right, right),
        in_specs=[pl.BlockSpec(memory_space=pl.ANY)] * 13,
        out_specs=[pl.BlockSpec(memory_space=pl.ANY)] * 7,
        scratch_shapes=scratch,
        compiler_params=pltpu.CompilerParams(
            collective_id=0, has_side_effects=True, vmem_limit_bytes=60 * 2**20
        ),
        name="grpo_step",
    )(
        hidden, cotangent,
        prompt_group_index.reshape(1, tokens), answer_token_mask.reshape(1, tokens),
        token_reward_order.reshape(1, tokens),
        source_lowdim_matrix, running_mean_source_matrix, running_variance_source_matrix,
        target_lowdim_matrix, running_mean_target_matrix, running_variance_target_matrix,
        frozen_down_weight, sampled_token_input,
    )


def solution(mesh):
    factor = P(None, "tensor")
    placed = (
        P("dp", "tensor"), P("dp", "tensor"), P("dp"), P("dp"), P("dp"),
        factor, factor, factor, factor, factor, factor, P("tensor", "dp"), factor,
    )
    owned = P("dp", "tensor")
    return jax.shard_map(
        shards,
        mesh=mesh,
        in_specs=placed,
        out_specs=(P(None, ("dp", "tensor")), owned, owned, owned, owned, owned, owned),
        check_vma=False,
    )
```

```python
import functools

import jax
import jax.numpy as jnp
from jax import lax
from jax.experimental import pallas as pl
from jax.experimental.pallas import tpu as pltpu
from jax.sharding import PartitionSpec as P

MESH = pl.DeviceIdType.MESH
F32 = jnp.float32
BF16 = jnp.bfloat16

adapter_scale = 2.0
bias_one = 1.0 - 0.9**10
bias_two = 1.0 - 0.999**10

BLOCKS = ((2, 0), (2, 1), (1, 0), (3, 1), (1, 1), (3, 0), (0, 1), (0, 0))
GAP_ONE, GAP_TWO = 3, 4
FAR = ((2, 1), (1, 1), (3, 1), (2, 0), (0, 1), (1, 0), (3, 0))


def contract(left, right, left_dim, right_dim):
    return lax.dot_general(
        left, right, (((left_dim,), (right_dim,)), ((), ())), preferred_element_type=F32
    )


def high_low(value):
    high = value.astype(BF16)
    return high, (value - high.astype(F32)).astype(BF16)


def quarters(value, width):
    return jnp.concatenate([value[:, q * width : (q + 1) * width] for q in range(4)], axis=0)


def kernel(
    nd, nt,
    hidden, cotangent, groups, mask, order, a_in, ma_in, va_in, b_in, mb_in, vb_in, weight, sampled,
    o_out, o_pa, o_ma, o_va, o_pb, o_mb, o_vb,
    hid, cot, grp, msk, odr, a, ma, va, b, mb, vb, w, x,
    stat, stat_r, s1, cr, cs, ar, full, g, gf, gs, gr, own, xa_s, xa_r, xall, bs, bc, bd,
    keep, give, got, part_s, part_r,
    lsem, wsem, pair_sem, got_sem, part_sem, part_rsem, b_sem, chain_sem,
):
    i = lax.axis_index("dp")
    t = lax.axis_index("tensor")
    core = lax.rem(t, 2)
    place = t // 4
    level = lax.rem(t // 2, 2)
    chips = nt // 2
    inner = hid.shape[1]
    width = cot.shape[1]
    quarter = gs.shape[2]
    n_tok = hid.shape[0]
    half_tok = n_tok // 2

    def tensor_peer(dx, dz, dc):
        return lax.rem(place + dx, 4) * 4 + lax.rem(level + dz, 2) * 2 + lax.rem(core + dc, 2)

    def dp_peer(dy, dz):
        return lax.rem(i // 4 + dz, 2) * 4 + lax.rem(lax.rem(i, 4) + dy, 4)

    same_core = [(dx, dz, 0) for dx, dz in FAR]
    tensor_all = [(dx, dz, dc) for dx, dz in FAR for dc in (1, 0)] + [(0, 0, 1)]

    def load(src, dst, n):
        copy = pltpu.make_async_copy(src, dst, lsem.at[n])
        copy.start()
        return copy

    small = [load(groups, grp, 0), load(mask, msk, 1), load(order, odr, 2)]
    b_load = load(b_in, b, 3)
    a_load = load(a_in, a, 4)
    cot_load = load(cotangent, cot, 5)
    pieces = 2
    piece = inner // pieces
    hid_load = []
    for n in range(pieces):
        cols = pl.ds(n * piece, piece)
        hid_load.append(load(hidden.at[:, cols], hid.at[:, cols], 6 + n))

    barrier = pltpu.get_barrier_semaphore()
    for dx, dz, dc in tensor_all:
        pl.semaphore_signal(
            barrier, inc=1, device_id={"tensor": tensor_peer(dx, dz, dc)}, device_id_type=MESH
        )
    for dy, dz in FAR:
        pl.semaphore_signal(barrier, inc=1, device_id={"dp": dp_peer(dy, dz)}, device_id_type=MESH)

    def w_load(s):
        dx, dz = BLOCKS[s]
        block = lax.rem(place + dx, 4) * 2 + lax.rem(level + dz, 2)
        cols = pl.ds(pl.multiple_of(block * 256, 256), 256)
        pltpu.make_async_copy(weight.at[:, cols], w.at[s], wsem.at[s]).start()

    for copy in small:
        copy.wait()
    mask_row = msk[...].astype(F32)
    rank_row = odr[...].astype(F32)
    n_groups = stat.shape[1]
    group_id = lax.broadcasted_iota(jnp.int32, (n_groups, n_tok), 0)
    member = jnp.where(group_id == grp[...], 1.0, 0.0).astype(BF16)
    row = lax.broadcasted_iota(jnp.int32, (8, n_tok), 0)
    weighted = mask_row * rank_row
    terms = jnp.where(
        row == 0, mask_row, jnp.where(row == 1, weighted, jnp.where(row == 2, weighted * rank_row, 0.0))
    )
    stat[...] = contract(terms.astype(BF16), member, 1, 1)

    b_load.wait()
    cot_load.wait()
    b_high, b_low = high_low(b[...])
    raw = contract(jnp.concatenate([b_high, b_low], axis=0), cot[...], 1, 1)
    s1[32:64, :] = raw[0:32] + raw[32:64]

    a_load.wait()
    a_half = a[...].astype(BF16)
    total = None
    for n in range(pieces):
        hid_load[n].wait()
        if n == 0:
            x_load = load(sampled, x, 8)
            for s in range(2):
                w_load(s)
        cols = slice(n * piece, (n + 1) * piece)
        part = contract(a_half[:, cols], hid[:, cols], 1, 1)
        total = part if total is None else total + part
    s1[0:32, :] = total
    for s in range(2, chips):
        w_load(s)
    late = [load(ma_in, ma, 9), load(va_in, va, 10), load(mb_in, mb, 11), load(vb_in, vb, 12)]

    pl.semaphore_wait(barrier, len(tensor_all) + len(FAR))

    def copy_to(src, dst, send, recv, peer):
        return pltpu.make_async_remote_copy(
            src_ref=src, dst_ref=dst, send_sem=send, recv_sem=recv, device_id=peer, device_id_type=MESH
        )

    def to_dp(src, dst, sems):
        for n, (dy, dz) in enumerate(FAR):
            peer = dp_peer(dy, dz)
            copy_to(
                src(peer), dst(n), chain_sem.at[sems], chain_sem.at[sems + 1], {"dp": peer}
            ).start()

    def to_tensor(src, dst, sems, peers):
        for n, (dx, dz, dc) in enumerate(peers):
            copy_to(
                src, dst(n), chain_sem.at[sems], chain_sem.at[sems + 1],
                {"tensor": tensor_peer(dx, dz, dc)},
            ).start()

    def arrived(ref, sems):
        pltpu.make_async_copy(ref, ref, chain_sem.at[sems + 1]).wait()

    def sent(ref, sems):
        pltpu.make_async_copy(ref, ref, chain_sem.at[sems]).wait()

    other = {"tensor": tensor_peer(0, 0, 1)}
    theirs = pl.ds(pl.multiple_of(32 - 32 * core, 32), 32)
    ours = pl.ds(pl.multiple_of(32 * core, 32), 32)
    chip_copy = copy_to(s1.at[theirs], cr, chain_sem.at[2], chain_sem.at[3], other)
    chip_copy.start()
    to_dp(lambda peer: stat, lambda n: stat_r.at[n], 0)
    chip_copy.wait_recv()
    chip_sum = s1[ours, :] + cr[...]
    s1[ours, :] = chip_sum
    cs[...] = chip_sum.astype(BF16)
    to_tensor(cs, lambda n: ar.at[n], 4, same_core)

    def pair_copy(s):
        return copy_to(give.at[s], got.at[s], pair_sem.at[s], got_sem.at[s], other)

    def compute(s, carry):
        pltpu.make_async_copy(weight.at[:, pl.ds(0, 256)], w.at[s], wsem.at[s]).wait()
        block = contract(x[...], w[s], 1, 0)
        first, second = block[:, :128], block[:, 128:]
        keep[s] = jnp.where(core == 0, first, second)
        give[s] = jnp.where(core == 0, second, first).astype(BF16)
        pair_copy(s).start()
        return carry

    def chip_total(s):
        pair_copy(s).wait_recv()
        return keep[s] + got[s].astype(F32)

    ahead = {"tensor": tensor_peer(1, 0, 0)}
    behind = {"tensor": tensor_peer(3, 0, 0)}
    across = {"tensor": tensor_peer(0, 1, 0)}
    routes = (ahead, behind, ahead, behind, ahead, behind, across)

    def part_copy(n):
        return copy_to(part_s.at[n], part_r.at[n], part_sem.at[n], part_rsem.at[n], routes[n])

    def forward(n, value):
        part_s[n] = value.astype(BF16)
        part_copy(n).start()

    def received(n):
        part_copy(n).wait_recv()
        return part_r[n].astype(F32)

    x_load.wait()
    lax.fori_loop(0, GAP_ONE, compute, 0)

    arrived(stat_r, 0)
    stats = stat[...]
    for d in range(nd - 1):
        stats = stats + stat_r[d]
    counts, sums, squares = stats[0:1], stats[1:2], stats[2:3]
    safe = jnp.maximum(counts, 1.0)
    mean = sums / safe
    spread = jnp.maximum(jnp.sqrt(jnp.maximum(squares / safe - mean * mean, 0.0)), 1.0)
    every = jnp.maximum(jnp.sum(counts, axis=1, keepdims=True), 1.0)
    table = jnp.zeros((8, n_groups), F32)
    row_g = lax.broadcasted_iota(jnp.int32, (8, n_groups), 0)
    for base, value in ((0, mean), (3, spread)):
        rest = value
        for n in range(3):
            term = rest.astype(BF16).astype(F32)
            table = jnp.where(row_g == base + n, term, table)
            rest = rest - term
    looked = contract(table.astype(BF16), member, 1, 0)
    mean_t = (looked[0:1] + looked[1:2]) + looked[2:3]
    spread_t = (looked[3:4] + looked[4:5]) + looked[5:6]
    coefficient = -mask_row * (rank_row - mean_t) / spread_t / every

    forward(0, chip_total(0))
    forward(1, chip_total(1))

    arrived(ar, 4)
    mine = s1[ours, :]
    for n in range(len(same_core)):
        mine = mine + ar[n].astype(F32)
    full[ours, :] = mine * coefficient
    full_copy = copy_to(full.at[ours], full.at[ours], chain_sem.at[6], chain_sem.at[7], other)
    full_copy.start()

    lax.fori_loop(GAP_ONE, GAP_TWO, compute, 0)

    full_copy.wait_recv()
    back = full[32:64, :].astype(BF16)
    p_high, p_low = high_low(full[0:32, :])
    g[:, 0:inner] = adapter_scale * contract(back, hid[...], 1, 0)
    right = contract(jnp.concatenate([p_high, p_low], axis=0), cot[...], 1, 0)
    g[:, inner : inner + width] = adapter_scale * (right[0:32] + right[32:64])
    g[:, inner + width :] = jnp.zeros((32, 4 * quarter - inner - width), F32)
    for r in range(nd):
        value = quarters(g[4 * r : 4 * r + 4, :], quarter)
        gf[r] = value
        gs[r] = value.astype(BF16)
    to_dp(lambda peer: gs.at[peer], lambda n: gr.at[n], 8)

    forward(2, chip_total(2) + received(0))
    forward(3, chip_total(3) + received(1))
    lax.fori_loop(GAP_TWO, chips, compute, 0)
    forward(4, chip_total(4))
    forward(5, chip_total(5))

    for copy in late:
        copy.wait()

    def own_rows(value_a, value_b, slot):
        rows = pl.ds(pl.multiple_of((i // 2) * 8, 8), 8)
        odd = lax.rem(i, 2) == 1

        def pick(ref):
            eight = ref[rows, :]
            return jnp.where(odd, eight[4:8], eight[0:4])

        pad = jnp.zeros((4, 4 * quarter - inner - width), F32)
        own[slot] = quarters(jnp.concatenate([pick(value_a), pick(value_b), pad], axis=1), quarter)

    own_rows(a, b, 0)
    own_rows(ma, mb, 1)
    own_rows(va, vb, 2)

    arrived(gr, 8)
    grad = gf[i]
    for n in range(nd - 1):
        grad = grad + gr[n].astype(F32)
    first = 0.9 * own[1] + 0.1 * grad
    second = 0.999 * own[2] + 0.001 * grad * grad
    param = own[0] - 0.004 * (first / bias_one) / (jnp.sqrt(second / bias_two) + 1e-08)
    a_send = param.astype(BF16)

    def split(value, left_ref, right_ref):
        for q in range(4):
            lo, hi = q * quarter, (q + 1) * quarter
            rows = value[4 * q : 4 * q + 4]
            if lo < inner and left_ref is not None:
                left_ref[:, lo : min(hi, inner)] = rows[:, : min(hi, inner) - lo]
            start, stop = max(lo, inner), min(hi, inner + width)
            if start < stop:
                right_ref[:, start - inner : stop - inner] = rows[:, start - lo : stop - lo]

    home = t // 2
    at_home = home == i
    split(a_send.astype(F32), None, bs)

    def home_copy():
        return copy_to(bs, bc.at[i], b_sem.at[0], b_sem.at[1], {"dp": home})

    @pl.when(jnp.logical_not(at_home))
    def _():
        home_copy().start()

    partial = None
    for q in range(4):
        cols = min(quarter, inner - q * quarter)
        if cols <= 0:
            continue
        part = contract(a_send[:, :cols], x[:, q * quarter : q * quarter + cols], 1, 1)
        part = part[4 * q : 4 * q + 4]
        partial = part if partial is None else partial + part
    xa_s[...] = jnp.concatenate([partial[:, :half_tok], partial[:, half_tok:]], axis=0)
    to_tensor(xa_s, lambda n: xa_r.at[n], 10, tensor_all)

    split(param, o_pa, o_pb)
    split(first, o_ma, o_mb)
    split(second, o_va, o_vb)

    forward(6, chip_total(6) + received(4) + received(3))
    keep[chips - 1] = chip_total(chips - 1) + received(2) + received(5)

    arrived(xa_r, 10)
    mine = xa_s[...]
    for n in range(len(tensor_all)):
        mine = mine + xa_r[n]
    xall[i] = mine
    to_dp(lambda peer: xall.at[i], lambda n: xall.at[i], 12)

    def column_copy(k):
        cols = pl.ds(128 * k, 128)
        return copy_to(
            bc.at[:, :, cols], bd, b_sem.at[2 + k], b_sem.at[10], {"tensor": 8 * core + k}
        )

    @pl.when(at_home)
    def _():
        pltpu.make_async_copy(bc.at[pl.ds(0, nd - 1)], bc.at[pl.ds(0, nd - 1)], b_sem.at[1]).wait()
        bc[i] = bs[...]
        for k in range(8):
            here = 8 * core + k == t

            @pl.when(jnp.logical_not(here))
            def _():
                column_copy(k).start()

            @pl.when(here)
            def _():
                bd[...] = bc[:, :, 128 * k : 128 * k + 128]

    keep[chips - 1] = keep[chips - 1] + received(6)

    @pl.when(2 * i + t // 8 != t)
    def _():
        pltpu.make_async_copy(bd, bd, b_sem.at[10]).wait()

    nothing = jnp.zeros((nd, 4, 128), F32)
    b_rows = bd[...]
    xall_bytes = xa_r.at[pl.ds(0, nd - 1)]
    arrived(xall_bytes, 12)
    z_high, z_low = high_low(xall[...].reshape(8 * nd, half_tok))
    z = jnp.concatenate([z_high, z_low], axis=0)
    for h in range(2):
        b_half = jnp.concatenate([nothing, b_rows] if h else [b_rows, nothing], axis=1)
        b_half = b_half.reshape(8 * nd, 128).astype(BF16)
        added = contract(z, jnp.concatenate([b_half, b_half], axis=0), 0, 0)
        rows = slice(h * half_tok, (h + 1) * half_tok)
        o_out[rows, :] = (keep[chips - 1, rows, :] + adapter_scale * added).astype(BF16)

    sent(stat_r, 0)
    chip_copy.wait_send()
    sent(ar, 4)
    full_copy.wait_send()
    sent(gr, 8)
    sent(xa_r, 10)
    sent(xall_bytes, 12)
    for s in range(chips):
        pair_copy(s).wait_send()
    for n in range(len(routes)):
        part_copy(n).wait_send()

    @pl.when(jnp.logical_not(at_home))
    def _():
        home_copy().wait_send()

    @pl.when(at_home)
    def _():
        for k in range(8):

            @pl.when(8 * core + k != t)
            def _():
                column_copy(k).wait_send()


def hand_over(*refs):
    *refs, sems = refs
    count = len(refs) // 2
    copies = [
        pltpu.make_async_copy(refs[n], refs[count + n], sems.at[n]) for n in range(count)
    ]
    for copy in copies:
        copy.start()
    for copy in copies:
        copy.wait()


def shards(
    hidden, cotangent, prompt_group_index, answer_token_mask, token_reward_order,
    source_lowdim_matrix, running_mean_source_matrix, running_variance_source_matrix,
    target_lowdim_matrix, running_mean_target_matrix, running_variance_target_matrix,
    frozen_down_weight, sampled_token_input,
):
    nd, nt = lax.axis_size("dp"), lax.axis_size("tensor")
    tokens, inner = hidden.shape
    width = cotangent.shape[1]
    rank = source_lowdim_matrix.shape[0]
    columns = frozen_down_weight.shape[1]
    rollout = sampled_token_input.shape[0]
    n_groups = tokens * nd // 8
    chips = nt // 2
    quarter = -(-(inner + width) // 512) * 128
    rows = rank // nd
    vmem, dma = pltpu.VMEM, pltpu.SemaphoreType.DMA
    i32 = jnp.int32
    scratch = [
        vmem((tokens, inner), BF16), vmem((tokens, width), BF16),
        vmem((1, tokens), i32), vmem((1, tokens), i32), vmem((1, tokens), i32),
        vmem((rank, inner), F32), vmem((rank, inner), F32), vmem((rank, inner), F32),
        vmem((rank, width), F32), vmem((rank, width), F32), vmem((rank, width), F32),
        vmem((chips, inner, 256), BF16), vmem((rollout, inner), BF16),
        vmem((8, n_groups), F32), vmem((nd - 1, 8, n_groups), F32),
        vmem((64, tokens), F32), vmem((32, tokens), F32), vmem((32, tokens), BF16),
        vmem((chips - 1, 32, tokens), BF16), vmem((64, tokens), F32),
        vmem((rank, 4 * quarter), F32), vmem((nd, 16, quarter), F32), vmem((nd, 16, quarter), BF16),
        vmem((nd - 1, 16, quarter), BF16), vmem((3, 16, quarter), F32),
        vmem((8, rollout // 2), F32), vmem((nt - 1, 8, rollout // 2), F32),
        vmem((nd, 8, rollout // 2), F32), vmem((rows, width), F32), vmem((nd, rows, width), F32),
        vmem((nd, rows, 128), F32),
        vmem((chips, rollout, 128), F32), vmem((chips, rollout, 128), BF16),
        vmem((chips, rollout, 128), BF16), vmem((7, rollout, 128), BF16),
        vmem((7, rollout, 128), BF16),
        dma((13,)), dma((chips,)), dma((chips,)), dma((chips,)), dma((7,)), dma((7,)), dma((11,)),
        dma((14,)),
    ]
    results = [((rollout, 128), BF16)] + [((rows, inner), F32)] * 3 + [((rows, width), F32)] * 3
    held = pl.pallas_call(
        functools.partial(kernel, nd, nt),
        out_shape=[vmem(shape, dtype) for shape, dtype in results],
        in_specs=[pl.BlockSpec(memory_space=pl.ANY)] * 13,
        out_specs=[pl.BlockSpec(memory_space=vmem)] * 7,
        scratch_shapes=scratch,
        compiler_params=pltpu.CompilerParams(
            collective_id=0, has_side_effects=True, vmem_limit_bytes=56 * 2**20
        ),
        name="grpo_step",
    )(
        hidden, cotangent,
        prompt_group_index.reshape(1, tokens), answer_token_mask.reshape(1, tokens),
        token_reward_order.reshape(1, tokens),
        source_lowdim_matrix, running_mean_source_matrix, running_variance_source_matrix,
        target_lowdim_matrix, running_mean_target_matrix, running_variance_target_matrix,
        frozen_down_weight, sampled_token_input,
    )
    held = [pltpu.with_memory_space_constraint(value, vmem) for value in held]
    return pl.pallas_call(
        hand_over,
        out_shape=tuple(jax.ShapeDtypeStruct(shape, dtype) for shape, dtype in results),
        in_specs=[pl.BlockSpec(memory_space=vmem)] * 7,
        out_specs=[pl.BlockSpec(memory_space=pl.ANY)] * 7,
        scratch_shapes=[dma((7,))],
        name="hand_over",
    )(*held)


def solution(mesh):
    factor = P(None, "tensor")
    placed = (
        P("dp", "tensor"), P("dp", "tensor"), P("dp"), P("dp"), P("dp"),
        factor, factor, factor, factor, factor, factor, P("tensor", "dp"), factor,
    )
    owned = P("dp", "tensor")
    return jax.shard_map(
        shards,
        mesh=mesh,
        in_specs=placed,
        out_specs=(P(None, ("dp", "tensor")), owned, owned, owned, owned, owned, owned),
        check_vma=False,
    )
```

```python
import functools

import jax
import jax.numpy as jnp
from jax import lax
from jax.experimental import pallas as pl
from jax.experimental.pallas import tpu as pltpu
from jax.sharding import PartitionSpec as P

MESH = pl.DeviceIdType.MESH
F32 = jnp.float32
BF16 = jnp.bfloat16

adapter_scale = 2.0
bias_one = 1.0 - 0.9**10
bias_two = 1.0 - 0.999**10

BLOCKS = ((2, 1), (3, 1), (1, 1), (0, 1), (2, 0), (1, 0), (3, 0), (0, 0))
PARTS = ((0, ()), (1, (0,)), (2, ()), (4, ()), (5, (3,)), (6, ()), (3, (1, 2)))
GAPS = (1, 3, 3, 4, 6, 8)
SENDS = ((), (), (0,), (2,), (1, 3), (4, 5, 6))
FAR = ((2, 1), (1, 1), (3, 1), (2, 0), (0, 1), (1, 0), (3, 0))
PLANE = (
    (2, 2), (2, 1), (2, 3), (1, 2), (3, 2), (1, 1), (1, 3), (3, 1), (3, 3), (2, 0), (0, 2), (1, 0),
    (3, 0), (0, 1), (0, 3),
)


def contract(left, right, left_dim, right_dim):
    return lax.dot_general(
        left, right, (((left_dim,), (right_dim,)), ((), ())), preferred_element_type=F32
    )


def high_low(value):
    high = value.astype(BF16)
    return high, (value - high.astype(F32)).astype(BF16)


def quarters(value, width):
    return jnp.concatenate([value[:, q * width : (q + 1) * width] for q in range(4)], axis=0)


def kernel(
    nd, nt,
    hidden, cotangent, groups, mask, order, a_in, ma_in, va_in, b_in, mb_in, vb_in, weight, sampled,
    o_out, o_pa, o_ma, o_va, o_pb, o_mb, o_vb,
    hid, cot, grp, msk, odr, a, ma, va, b, mb, vb, w, x, xt,
    stat, stat_r, s1, cr, cs, ar, full, ga, gaf, gas, gar, gb, gbf, gbs, gbr, own_a, own_b,
    xa_s, xa_r, xall, bs, bc, bd, keep, give, got, part_s, part_r,
    lsem, wsem, pair_sem, got_sem, part_sem, part_rsem, b_sem, chain_sem,
):
    i = lax.axis_index("dp")
    t = lax.axis_index("tensor")
    core = lax.rem(t, 2)
    place = t // 4
    level = lax.rem(t // 2, 2)
    chips = nt // 2
    inner = hid.shape[1]
    width = cot.shape[1]
    quarter = gas.shape[2]
    quarter_b = gbs.shape[2]
    n_tok = hid.shape[0]

    def tensor_peer(dx, dz, dc):
        return lax.rem(place + dx, 4) * 4 + lax.rem(level + dz, 2) * 2 + lax.rem(core + dc, 2)

    def dp_peer(dy, dz):
        return lax.rem(i // 4 + dz, 2) * 4 + lax.rem(lax.rem(i, 4) + dy, 4)

    def plane_peer(dy, dz):
        z = lax.rem((i // 4) * 2 + level + dz, 4)
        return {
            "dp": (z // 2) * 4 + lax.rem(lax.rem(i, 4) + dy, 4),
            "tensor": place * 4 + lax.rem(z, 2) * 2 + core,
        }

    same_core = [(dx, dz, 0) for dx, dz in FAR]
    tensor_all = [(dx, dz, dc) for dx, dz in FAR for dc in (1, 0)] + [(0, 0, 1)]
    same_level = [(dx, 0, dc) for dc in (1, 0) for dx in (2, 1, 3)] + [(0, 0, 1)]

    def load(src, dst, n):
        copy = pltpu.make_async_copy(src, dst, lsem.at[n])
        copy.start()
        return copy

    b_load = load(b_in, b, 3)
    cot_load = load(cotangent, cot, 5)

    barrier = pltpu.get_barrier_semaphore()
    for dy, dz in PLANE:
        pl.semaphore_signal(barrier, inc=1, device_id=plane_peer(dy, dz), device_id_type=MESH)
    for dx, dz, dc in tensor_all:
        pl.semaphore_signal(
            barrier, inc=1, device_id={"tensor": tensor_peer(dx, dz, dc)}, device_id_type=MESH
        )

    def w_load(s):
        dx, dz = BLOCKS[s]
        block = lax.rem(place + dx, 4) * 2 + lax.rem(level + dz, 2)
        cols = pl.ds(pl.multiple_of(block * 256, 256), 256)
        pltpu.make_async_copy(weight.at[:, cols], w.at[s], wsem.at[s]).start()

    small = [load(groups, grp, 0), load(mask, msk, 1), load(order, odr, 2)]
    a_load = load(a_in, a, 4)
    pieces = (0, 1280, 2304, inner)
    hid_load = []
    for n in range(len(pieces) - 1):
        cols = pl.ds(pieces[n], pieces[n + 1] - pieces[n])
        hid_load.append(load(hidden.at[:, cols], hid.at[:, cols], 6 + n))

    x_load = load(sampled, x, 9)
    for s in range(2):
        w_load(s)

    for copy in small:
        copy.wait()
    mask_row = msk[...].astype(F32)
    rank_row = odr[...].astype(F32)
    n_groups = stat.shape[1]
    group_id = lax.broadcasted_iota(jnp.int32, (n_groups, n_tok), 0)
    member = jnp.where(group_id == grp[...], 1.0, 0.0).astype(BF16)
    row = lax.broadcasted_iota(jnp.int32, (8, n_tok), 0)
    weighted = mask_row * rank_row
    terms = jnp.where(
        row == 0, mask_row, jnp.where(row == 1, weighted, jnp.where(row == 2, weighted * rank_row, 0.0))
    )
    stat[...] = contract(terms.astype(BF16), member, 1, 1)[0:4]

    b_load.wait()
    b_high, b_low = high_low(b[...])
    cot_load.wait()
    raw = contract(jnp.concatenate([b_high, b_low], axis=0), cot[...], 1, 1)
    s1[1] = raw[0:32] + raw[32:64]


    def copy_to(src, dst, send, recv, peer):
        return pltpu.make_async_remote_copy(
            src_ref=src, dst_ref=dst, send_sem=send, recv_sem=recv, device_id=peer, device_id_type=MESH
        )

    def to_dp(src, dst, sems):
        for n, (dy, dz) in enumerate(FAR):
            peer = dp_peer(dy, dz)
            copy_to(
                src(peer), dst(n), chain_sem.at[sems], chain_sem.at[sems + 1], {"dp": peer}
            ).start()

    def to_tensor(src, dst, sems, peers):
        for n, (dx, dz, dc) in enumerate(peers):
            copy_to(
                src, dst(n), chain_sem.at[sems], chain_sem.at[sems + 1],
                {"tensor": tensor_peer(dx, dz, dc)},
            ).start()

    def arrived(ref, sems):
        pltpu.make_async_copy(ref, ref, chain_sem.at[sems + 1]).wait()

    def sent(ref, sems):
        pltpu.make_async_copy(ref, ref, chain_sem.at[sems]).wait()

    other = {"tensor": tensor_peer(0, 0, 1)}
    theirs = pl.ds(pl.multiple_of(16 - 16 * core, 16), 16)
    ours = pl.ds(pl.multiple_of(16 * core, 16), 16)

    def chip_copy(n):
        return copy_to(
            s1.at[n, theirs], cr.at[n], chain_sem.at[12 + 2 * n], chain_sem.at[13 + 2 * n], other
        )

    def full_copy(n):
        return copy_to(
            full.at[n, ours], full.at[n, ours], chain_sem.at[16 + 2 * n], chain_sem.at[17 + 2 * n], other
        )

    def to_chips(n):
        chip_copy(n).wait_recv()
        chip_sum = s1[n, ours, :] + cr[n]
        s1[n, ours, :] = chip_sum
        cs[n] = chip_sum.astype(BF16)
        to_tensor(cs.at[n], lambda m: ar.at[n, m], 2 + 2 * n, same_core)

    def from_chips(n):
        arrived(ar.at[n], 2 + 2 * n)
        mine = s1[n, ours, :]
        for m in range(len(same_core)):
            mine = mine + ar[n, m].astype(F32)
        full[n, ours, :] = mine
        full_copy(n).start()

    pl.semaphore_wait(barrier, len(tensor_all) + len(PLANE))
    chip_copy(1).start()

    to_dp(lambda peer: stat, lambda n: stat_r.at[n], 0)
    to_chips(1)

    a_load.wait()
    a_half = a[...].astype(BF16)
    total = None
    for n, copy in enumerate(hid_load):
        copy.wait()
        cols = slice(pieces[n], pieces[n + 1])
        part = contract(a_half[:, cols], hid[:, cols], 1, 1)
        total = part if total is None else total + part
    s1[0] = total
    chip_copy(0).start()
    for s in range(2, 4):
        w_load(s)
    late = [load(ma_in, ma, 10), load(va_in, va, 11), load(mb_in, mb, 12), load(vb_in, vb, 13)]
    for s in range(4, chips):
        w_load(s)

    def pair_copy(s):
        return copy_to(give.at[s], got.at[s], pair_sem.at[s], got_sem.at[s], other)

    def compute(s, carry):
        pltpu.make_async_copy(weight.at[:, pl.ds(0, 256)], w.at[s], wsem.at[s]).wait()
        block = contract(x[...], w[s], 1, 0)
        first, second = block[:, :128], block[:, 128:]
        keep[s] = jnp.where(core == 0, first, second)
        give[s] = jnp.where(core == 0, second, first).astype(BF16)
        pair_copy(s).start()
        return carry

    def chip_total(s):
        pair_copy(s).wait_recv()
        return keep[s] + got[s].astype(F32)

    ahead = {"tensor": tensor_peer(1, 0, 0)}
    behind = {"tensor": tensor_peer(3, 0, 0)}
    across = {"tensor": tensor_peer(0, 1, 0)}
    routes = (behind, behind, ahead, ahead, ahead, behind, across)

    def part_copy(n):
        return copy_to(part_s.at[n], part_r.at[n], part_sem.at[n], part_rsem.at[n], routes[n])

    def forward(n, value):
        part_s[n] = value.astype(BF16)
        part_copy(n).start()

    def received(n):
        part_copy(n).wait_recv()
        return part_r[n].astype(F32)

    def run(gap):
        first = GAPS[gap - 1] if gap else 0
        if first == 0 and GAPS[gap]:
            x_load.wait()
        if first < GAPS[gap]:
            lax.fori_loop(first, GAPS[gap], compute, 0)
        for n in SENDS[gap]:
            block, parts = PARTS[n]
            value = chip_total(block)
            for m in parts:
                value = value + received(m)
            forward(n, value)

    run(0)
    to_chips(0)
    run(1)

    from_chips(1)
    arrived(stat_r, 0)
    stats = stat[...]
    for d in range(nd - 1):
        stats = stats + stat_r[d]
    counts, sums, squares = stats[0:1], stats[1:2], stats[2:3]
    safe = jnp.maximum(counts, 1.0)
    mean = sums / safe
    spread = jnp.maximum(jnp.sqrt(jnp.maximum(squares / safe - mean * mean, 0.0)), 1.0)
    every = jnp.maximum(jnp.sum(counts, axis=1, keepdims=True), 1.0)
    table = jnp.zeros((8, n_groups), F32)
    row_g = lax.broadcasted_iota(jnp.int32, (8, n_groups), 0)
    for base, value in ((0, mean), (3, spread)):
        rest = value
        for n in range(3):
            term = rest.astype(BF16).astype(F32)
            table = jnp.where(row_g == base + n, term, table)
            rest = rest - term
    looked = contract(table.astype(BF16), member, 1, 0)
    mean_t = (looked[0:1] + looked[1:2]) + looked[2:3]
    spread_t = (looked[3:4] + looked[4:5]) + looked[5:6]
    coefficient = -mask_row * (rank_row - mean_t) / spread_t / every

    full_copy(1).wait_recv()
    ga[:, 0:inner] = adapter_scale * contract((full[1] * coefficient).astype(BF16), hid[...], 1, 0)
    ga[:, inner:] = jnp.zeros((32, 4 * quarter - inner), F32)
    for r in range(nd):
        value = quarters(ga[4 * r : 4 * r + 4, :], quarter)
        gaf[r] = value
        gas[r] = value.astype(BF16)
    to_dp(lambda peer: gas.at[peer], lambda n: gar.at[n], 6)

    from_chips(0)
    run(2)
    run(3)

    full_copy(0).wait_recv()
    p_high, p_low = high_low(full[0] * coefficient)
    right = contract(jnp.concatenate([p_high, p_low], axis=0), cot[...], 1, 0)
    gb[...] = adapter_scale * (right[0:32] + right[32:64])
    for r in range(nd):
        value = quarters(gb[4 * r : 4 * r + 4, :], quarter_b)
        gbf[r] = value
        gbs[r] = value.astype(BF16)
    to_dp(lambda peer: gbs.at[peer], lambda n: gbr.at[n], 20)

    for copy in late:
        copy.wait()

    def own_rows(ref, quarter):
        rows = pl.ds(pl.multiple_of((i // 2) * 8, 8), 8)
        eight = ref[rows, :]
        four = jnp.where(lax.rem(i, 2) == 1, eight[4:8], eight[0:4])
        pad = 4 * quarter - four.shape[1]
        if pad:
            four = jnp.concatenate([four, jnp.zeros((4, pad), F32)], axis=1)
        return quarters(four, quarter)

    for n, (ref_a, ref_b) in enumerate(((a, b), (ma, mb), (va, vb))):
        own_a[n] = own_rows(ref_a, quarter)
        own_b[n] = own_rows(ref_b, quarter_b)

    run(4)

    def adam(own, grad, received_grads):
        for n in range(nd - 1):
            grad = grad + received_grads[n].astype(F32)
        first = 0.9 * own[1] + 0.1 * grad
        second = 0.999 * own[2] + 0.001 * grad * grad
        param = own[0] - 0.004 * (first / bias_one) / (jnp.sqrt(second / bias_two) + 1e-08)
        return param, first, second

    def split(value, ref, quarter):
        columns = ref.shape[1]
        for q in range(4):
            lo, hi = q * quarter, min((q + 1) * quarter, columns)
            ref[:, lo:hi] = value[4 * q : 4 * q + 4, : hi - lo]

    for n in range(inner // 256):
        xt[256 * n : 256 * (n + 1), :] = x[:, 256 * n : 256 * (n + 1)].T
    arrived(gar, 6)
    adam_a = adam(own_a, gaf[i], gar)
    a_send = adam_a[0].astype(BF16)
    partial = None
    for q in range(4):
        lo, hi = q * quarter, min((q + 1) * quarter, inner)
        part = contract(a_send[:, : hi - lo], xt[lo:hi, :], 1, 0)
        part = part[4 * q : 4 * q + 4]
        partial = part if partial is None else partial + part
    partial = quarters(partial, n_tok // 4)
    xa_s[...] = partial.astype(BF16)
    to_tensor(xa_s, lambda n: xa_r.at[n], 8, same_level)

    arrived(gbr, 20)
    adam_b = adam(own_b, gbf[i], gbr)
    home = t // 2
    at_home = home == i
    split(adam_b[0].astype(BF16).astype(F32), bs, quarter_b)

    def home_copy():
        return copy_to(bs, bc.at[i], b_sem.at[0], b_sem.at[1], {"dp": home})

    @pl.when(jnp.logical_not(at_home))
    def _():
        home_copy().start()

    for value, ref in zip(adam_a, (o_pa, o_ma, o_va)):
        split(value, ref, quarter)
    for value, ref in zip(adam_b, (o_pb, o_mb, o_vb)):
        split(value, ref, quarter_b)

    run(5)

    arrived(xa_r, 8)
    mine = partial
    for n in range(len(same_level)):
        mine = mine + xa_r[n].astype(F32)
    slot = level * nd + i
    xall[slot] = mine.astype(BF16)
    for dy, dz in PLANE:
        copy_to(
            xall.at[slot], xall.at[slot], chain_sem.at[10], chain_sem.at[11], plane_peer(dy, dz)
        ).start()

    def column_copy(k):
        cols = pl.ds(128 * k, 128)
        return copy_to(
            bc.at[:, :, cols], bd, b_sem.at[2 + k], b_sem.at[10], {"tensor": 8 * core + k}
        )

    @pl.when(at_home)
    def _():
        pltpu.make_async_copy(bc.at[pl.ds(0, nd - 1)], bc.at[pl.ds(0, nd - 1)], b_sem.at[1]).wait()
        bc[i] = bs[...]
        for k in range(8):
            here = 8 * core + k == t

            @pl.when(jnp.logical_not(here))
            def _():
                column_copy(k).start()

            @pl.when(here)
            def _():
                bd[...] = bc[:, :, 128 * k : 128 * k + 128]

    keep[chips - 1] = chip_total(chips - 1) + received(4) + received(5) + received(6)

    @pl.when(2 * i + t // 8 != t)
    def _():
        pltpu.make_async_copy(bd, bd, b_sem.at[10]).wait()

    b_rows = bd[...]
    b_rows = jnp.concatenate([b_rows] * 4, axis=1).reshape(16 * nd, 128)
    row_b = lax.rem(lax.broadcasted_iota(jnp.int32, (16 * nd, 128), 0), 16) // 4
    b_parts = [jnp.where(row_b == q, b_rows, 0.0).astype(BF16) for q in range(4)]
    xall_bytes = xall.at[pl.ds(0, len(PLANE))]
    arrived(xall_bytes, 10)
    z = xall[...].reshape(32 * nd, n_tok // 4)
    for q in range(4):
        added = contract(z, jnp.concatenate([b_parts[q], b_parts[q]], axis=0), 0, 0)
        rows = slice(q * (n_tok // 4), (q + 1) * (n_tok // 4))
        o_out[rows, :] = (keep[chips - 1, rows, :] + adapter_scale * added).astype(BF16)

    sent(stat_r, 0)
    for n in range(2):
        chip_copy(n).wait_send()
        sent(ar.at[n], 2 + 2 * n)
        full_copy(n).wait_send()
    sent(gar, 6)
    sent(gbr, 20)
    sent(xa_r, 8)
    sent(xall_bytes, 10)
    for s in range(chips):
        pair_copy(s).wait_send()
    for n in range(len(routes)):
        part_copy(n).wait_send()

    @pl.when(jnp.logical_not(at_home))
    def _():
        home_copy().wait_send()

    @pl.when(at_home)
    def _():
        for k in range(8):

            @pl.when(8 * core + k != t)
            def _():
                column_copy(k).wait_send()


def hand_over(*refs):
    *refs, sems = refs
    count = len(refs) // 2
    copies = [
        pltpu.make_async_copy(refs[n], refs[count + n], sems.at[n]) for n in range(count)
    ]
    for copy in copies:
        copy.start()
    for copy in copies:
        copy.wait()


def shards(
    hidden, cotangent, prompt_group_index, answer_token_mask, token_reward_order,
    source_lowdim_matrix, running_mean_source_matrix, running_variance_source_matrix,
    target_lowdim_matrix, running_mean_target_matrix, running_variance_target_matrix,
    frozen_down_weight, sampled_token_input,
):
    nd, nt = lax.axis_size("dp"), lax.axis_size("tensor")
    tokens, inner = hidden.shape
    width = cotangent.shape[1]
    rank = source_lowdim_matrix.shape[0]
    columns = frozen_down_weight.shape[1]
    rollout = sampled_token_input.shape[0]
    n_groups = tokens * nd // 8
    chips = nt // 2
    quarter, quarter_b = -(-inner // 512) * 128, -(-width // 512) * 128
    rows = rank // nd
    vmem, dma = pltpu.VMEM, pltpu.SemaphoreType.DMA
    i32 = jnp.int32
    scratch = [
        vmem((tokens, inner), BF16), vmem((tokens, width), BF16),
        vmem((1, tokens), i32), vmem((1, tokens), i32), vmem((1, tokens), i32),
        vmem((rank, inner), F32), vmem((rank, inner), F32), vmem((rank, inner), F32),
        vmem((rank, width), F32), vmem((rank, width), F32), vmem((rank, width), F32),
        vmem((chips, inner, 256), BF16), vmem((rollout, inner), BF16),
        vmem((inner, rollout), BF16),
        vmem((4, n_groups), F32), vmem((nd - 1, 4, n_groups), F32),
        vmem((2, 32, tokens), F32), vmem((2, 16, tokens), F32), vmem((2, 16, tokens), BF16),
        vmem((2, chips - 1, 16, tokens), BF16), vmem((2, 32, tokens), F32),
        vmem((rank, 4 * quarter), F32), vmem((nd, 16, quarter), F32), vmem((nd, 16, quarter), BF16),
        vmem((nd - 1, 16, quarter), BF16),
        vmem((rank, 4 * quarter_b), F32), vmem((nd, 16, quarter_b), F32),
        vmem((nd, 16, quarter_b), BF16), vmem((nd - 1, 16, quarter_b), BF16),
        vmem((3, 16, quarter), F32), vmem((3, 16, quarter_b), F32),
        vmem((16, rollout // 4), BF16), vmem((chips - 1, 16, rollout // 4), BF16),
        vmem((2 * nd, 16, rollout // 4), BF16), vmem((rows, width), F32), vmem((nd, rows, width), F32),
        vmem((nd, rows, 128), F32),
        vmem((chips, rollout, 128), F32), vmem((chips, rollout, 128), BF16),
        vmem((chips, rollout, 128), BF16), vmem((7, rollout, 128), BF16),
        vmem((7, rollout, 128), BF16),
        dma((14,)), dma((chips,)), dma((chips,)), dma((chips,)), dma((7,)), dma((7,)), dma((11,)),
        dma((22,)),
    ]
    results = [((rollout, 128), BF16)] + [((rows, inner), F32)] * 3 + [((rows, width), F32)] * 3
    held = pl.pallas_call(
        functools.partial(kernel, nd, nt),
        out_shape=[vmem(shape, dtype) for shape, dtype in results],
        in_specs=[pl.BlockSpec(memory_space=pl.ANY)] * 13,
        out_specs=[pl.BlockSpec(memory_space=vmem)] * 7,
        scratch_shapes=scratch,
        compiler_params=pltpu.CompilerParams(
            collective_id=0, has_side_effects=True, vmem_limit_bytes=56 * 2**20
        ),
        name="grpo_step",
    )(
        hidden, cotangent,
        prompt_group_index.reshape(1, tokens), answer_token_mask.reshape(1, tokens),
        token_reward_order.reshape(1, tokens),
        source_lowdim_matrix, running_mean_source_matrix, running_variance_source_matrix,
        target_lowdim_matrix, running_mean_target_matrix, running_variance_target_matrix,
        frozen_down_weight, sampled_token_input,
    )
    held = [pltpu.with_memory_space_constraint(value, vmem) for value in held]
    return pl.pallas_call(
        hand_over,
        out_shape=tuple(jax.ShapeDtypeStruct(shape, dtype) for shape, dtype in results),
        in_specs=[pl.BlockSpec(memory_space=vmem)] * 7,
        out_specs=[pl.BlockSpec(memory_space=pl.ANY)] * 7,
        scratch_shapes=[dma((7,))],
        name="hand_over",
    )(*held)


def solution(mesh):
    factor = P(None, "tensor")
    placed = (
        P("dp", "tensor"), P("dp", "tensor"), P("dp"), P("dp"), P("dp"),
        factor, factor, factor, factor, factor, factor, P("tensor", "dp"), factor,
    )
    owned = P("dp", "tensor")
    return jax.shard_map(
        shards,
        mesh=mesh,
        in_specs=placed,
        out_specs=(P(None, ("dp", "tensor")), owned, owned, owned, owned, owned, owned),
        check_vma=False,
    )
```

```python
import functools
import math

import jax
import jax.numpy as jnp
from jax import lax
from jax.experimental import pallas as pl
from jax.experimental.pallas import tpu as pltpu
from jax.sharding import PartitionSpec as P

MESH = pl.DeviceIdType.MESH
F32 = jnp.float32
BF16 = jnp.bfloat16

adapter_scale = 2.0
bias_one = 1.0 - 0.9**10
bias_two = 1.0 - 0.999**10

BLOCKS = ((2, 1), (3, 1), (1, 1), (0, 1), (2, 0), (1, 0), (3, 0), (0, 0))
PARTS = ((0, ()), (1, (0,)), (2, ()), (4, ()), (5, (3,)), (6, ()), (3, (1, 2)))
GAPS = (1, 3, 3, 4, 6, 8)
ARRIVALS = ((0, 1), (1, 3), (3, 4), (4, 7))
SENDS = ((), (), (0,), (2,), (3, 1), (6, 4, 5))
FAR = ((2, 1), (1, 1), (3, 1), (2, 0), (0, 1), (1, 0), (3, 0))
PLANE = (
    (2, 2), (2, 1), (2, 3), (1, 2), (3, 2), (1, 1), (1, 3), (3, 1), (3, 3), (2, 0), (0, 2), (1, 0),
    (3, 0), (0, 1), (0, 3),
)


def contract(left, right, left_dim, right_dim):
    return lax.dot_general(
        left, right, (((left_dim,), (right_dim,)), ((), ())), preferred_element_type=F32
    )


def high_low(value):
    high = value.astype(BF16)
    return high, (value - high.astype(F32)).astype(BF16)


def quarters(value, width):
    return jnp.concatenate([value[:, q * width : (q + 1) * width] for q in range(4)], axis=0)


def kernel(
    nd, nt,
    hidden, cotangent, groups, mask, order, a_in, ma_in, va_in, b_in, mb_in, vb_in, weight, sampled,
    o_out, o_pa, o_ma, o_va, o_pb, o_mb, o_vb,
    hid, cot, ints, a, mva, b, mvb, w, x, xt,
    stat, stat_r, s1, cr, cs, ar, full, ga, gaf, gas, gar, gb, gbf, gbs, gbr, own_a, own_b,
    xa_s, xa_r, xall, bs, bc, bd, keep, give, got, part_s, part_r,
    lsem, out_sem, in_sem,
):
    i = lax.axis_index("dp")
    t = lax.axis_index("tensor")
    core = lax.rem(t, 2)
    place = t // 4
    level = lax.rem(t // 2, 2)
    chips = nt // 2
    inner = hid.shape[1]
    width = cot.shape[1]
    quarter = gas.shape[2]
    quarter_b = gbs.shape[2]
    n_tok = hid.shape[0]

    def tensor_peer(dx, dz, dc):
        return lax.rem(place + dx, 4) * 4 + lax.rem(level + dz, 2) * 2 + lax.rem(core + dc, 2)

    def dp_peer(dy, dz):
        return lax.rem(i // 4 + dz, 2) * 4 + lax.rem(lax.rem(i, 4) + dy, 4)

    def plane_peer(dy, dz):
        z = lax.rem((i // 4) * 2 + level + dz, 4)
        return {
            "dp": (z // 2) * 4 + lax.rem(lax.rem(i, 4) + dy, 4),
            "tensor": place * 4 + lax.rem(z, 2) * 2 + core,
        }

    same_core = [(dx, dz, 0) for dx, dz in FAR]
    tensor_all = [(dx, dz, dc) for dx, dz in FAR for dc in (1, 0)] + [(0, 0, 1)]
    same_level = [(dx, 0, dc) for dc in (1, 0) for dx in (2, 1, 3)] + [(0, 0, 1)]

    def landed(ref, sem):
        pltpu.make_async_copy(ref, ref, sem).wait()

    def load(src, dst, n):
        copy = pltpu.make_async_copy(src, dst, lsem.at[n])
        copy.start()
        return copy

    b_load = load(b_in, b, 1)
    cot_load = load(cotangent, cot, 2)

    barrier = pltpu.get_barrier_semaphore()
    for dy, dz in PLANE:
        pl.semaphore_signal(barrier, inc=1, device_id=plane_peer(dy, dz), device_id_type=MESH)
    for dx, dz, dc in tensor_all:
        pl.semaphore_signal(
            barrier, inc=1, device_id={"tensor": tensor_peer(dx, dz, dc)}, device_id_type=MESH
        )

    def w_load(s):
        dx, dz = BLOCKS[s]
        block = lax.rem(place + dx, 4) * 2 + lax.rem(level + dz, 2)
        cols = pl.ds(pl.multiple_of(block * 256, 256), 256)
        load(weight.at[:, cols], w.at[s], 10 + s)

    for n, source in enumerate((groups, mask, order)):
        load(source, ints.at[n], 0)
    a_load = load(a_in, a, 3)
    pieces = (0, 1280, 2304, inner)
    hid_load = []
    for n in range(len(pieces) - 1):
        cols = pl.ds(pieces[n], pieces[n + 1] - pieces[n])
        hid_load.append(load(hidden.at[:, cols], hid.at[:, cols], 4 + n))

    x_load = load(sampled, x, 7)
    for s in range(2):
        w_load(s)

    landed(ints, lsem.at[0])
    mask_row = ints[1].astype(F32)
    rank_row = ints[2].astype(F32)
    n_groups = stat.shape[1]
    group_id = lax.broadcasted_iota(jnp.int32, (n_groups, n_tok), 0)
    member = jnp.where(group_id == ints[0], 1.0, 0.0).astype(BF16)
    row = lax.broadcasted_iota(jnp.int32, (8, n_tok), 0)
    weighted = mask_row * rank_row
    terms = jnp.where(
        row == 0, mask_row, jnp.where(row == 1, weighted, jnp.where(row == 2, weighted * rank_row, 0.0))
    )
    stat[...] = contract(terms.astype(BF16), member, 1, 1)[0:4]

    b_load.wait()
    b_high, b_low = high_low(b[...])
    cot_load.wait()
    raw = contract(jnp.concatenate([b_high, b_low], axis=0), cot[...], 1, 1)
    s1[1] = raw[0:32] + raw[32:64]

    def copy_to(src, dst, send, recv, peer):
        return pltpu.make_async_remote_copy(
            src_ref=src, dst_ref=dst, send_sem=send, recv_sem=recv, device_id=peer, device_id_type=MESH
        )

    pushed = []

    def push(src, dst, n, peer, times=1):
        pushed.append(times * math.prod(src.shape) * jnp.dtype(src.dtype).itemsize)
        return copy_to(src, dst, out_sem.at[0], in_sem.at[n], peer)

    def to_dp(src, dst, n):
        for m, (dy, dz) in enumerate(FAR):
            peer = dp_peer(dy, dz)
            push(src(peer), dst(m), n, {"dp": peer}).start()

    def to_tensor(src, dst, n, peers):
        for m, (dx, dz, dc) in enumerate(peers):
            push(src, dst(m), n, {"tensor": tensor_peer(dx, dz, dc)}).start()

    other = {"tensor": tensor_peer(0, 0, 1)}
    theirs = pl.ds(pl.multiple_of(16 - 16 * core, 16), 16)
    ours = pl.ds(pl.multiple_of(16 * core, 16), 16)

    def to_chips(n):
        landed(cr.at[n], in_sem.at[3 + n])
        chip_sum = s1[n, ours, :] + cr[n]
        s1[n, ours, :] = chip_sum
        cs[n] = chip_sum.astype(BF16)
        to_tensor(cs.at[n], lambda m: ar.at[n, m], 1 + n, same_core)

    def from_chips(n):
        landed(ar.at[n], in_sem.at[1 + n])
        mine = s1[n, ours, :]
        for m in range(len(same_core)):
            mine = mine + ar[n, m].astype(F32)
        full[n, ours, :] = mine
        push(full.at[n, ours], full.at[n, ours], 5 + n, other).start()

    pl.semaphore_wait(barrier, len(tensor_all) + len(PLANE))
    push(s1.at[1, theirs], cr.at[1], 4, other).start()
    to_dp(lambda peer: stat, lambda n: stat_r.at[n], 0)
    to_chips(1)

    a_load.wait()
    a_half = a[...].astype(BF16)
    total = None
    for n, copy in enumerate(hid_load):
        copy.wait()
        cols = slice(pieces[n], pieces[n + 1])
        part = contract(a_half[:, cols], hid[:, cols], 1, 1)
        total = part if total is None else total + part
    s1[0] = total
    push(s1.at[0, theirs], cr.at[0], 3, other).start()
    for s in range(2, 4):
        w_load(s)
    for n, (source_a, source_b) in enumerate(((ma_in, mb_in), (va_in, vb_in))):
        load(source_a, mva.at[n], 8)
        load(source_b, mvb.at[n], 9)
    for s in range(4, chips):
        w_load(s)

    taken = set()

    def compute(lo, hi):
        def body(s, carry):
            landed(w.at[s], lsem.at[10 + s])
            block = contract(x[...], w[s], 1, 0)
            first, second = block[:, :128], block[:, 128:]
            keep[s] = jnp.where(core == 0, first, second)
            give[s] = jnp.where(core == 0, second, first).astype(BF16)
            copy_to(give.at[s], got.at[s], out_sem.at[0], in_sem.at[13 + s], other).start()
            return carry

        lax.fori_loop(lo, hi, body, 0)
        pushed.append((hi - lo) * math.prod(give.shape[1:]) * 2)

    def once(key, ref, sem):
        if key not in taken:
            landed(ref, sem)
        taken.add(key)

    def chip_total(s):
        landed(got.at[s], in_sem.at[13 + s])
        return keep[s] + got[s].astype(F32)

    ahead = {"tensor": tensor_peer(1, 0, 0)}
    behind = {"tensor": tensor_peer(3, 0, 0)}
    across = {"tensor": tensor_peer(0, 1, 0)}
    routes = (behind, behind, ahead, ahead, ahead, behind, across)

    def arrival(n):
        return [lo <= n < hi for lo, hi in ARRIVALS].index(True)

    def forward(n, value):
        part_s[n] = value.astype(BF16)
        push(part_s.at[n], part_r.at[n], 21 + arrival(n), routes[n]).start()

    def received(n):
        m = arrival(n)
        lo, hi = ARRIVALS[m]
        once(("part", m), part_r.at[pl.ds(lo, hi - lo)], in_sem.at[21 + m])
        return part_r[n].astype(F32)

    def run(gap):
        first = GAPS[gap - 1] if gap else 0
        if first < GAPS[gap]:
            if first == 0:
                x_load.wait()
            compute(first, GAPS[gap])
        for n in SENDS[gap]:
            block, parts = PARTS[n]
            value = chip_total(block)
            for m in parts:
                value = value + received(m)
            forward(n, value)

    run(0)
    to_chips(0)
    run(1)

    from_chips(1)
    landed(stat_r, in_sem.at[0])
    stats = stat[...]
    for d in range(nd - 1):
        stats = stats + stat_r[d]
    counts, sums, squares = stats[0:1], stats[1:2], stats[2:3]
    safe = jnp.maximum(counts, 1.0)
    mean = sums / safe
    spread = jnp.maximum(jnp.sqrt(jnp.maximum(squares / safe - mean * mean, 0.0)), 1.0)
    every = jnp.maximum(jnp.sum(counts, axis=1, keepdims=True), 1.0)
    table = jnp.zeros((8, n_groups), F32)
    row_g = lax.broadcasted_iota(jnp.int32, (8, n_groups), 0)
    for base, value in ((0, mean), (3, spread)):
        rest = value
        for n in range(3):
            term = rest.astype(BF16).astype(F32)
            table = jnp.where(row_g == base + n, term, table)
            rest = rest - term
    looked = contract(table.astype(BF16), member, 1, 0)
    mean_t = (looked[0:1] + looked[1:2]) + looked[2:3]
    spread_t = (looked[3:4] + looked[4:5]) + looked[5:6]
    coefficient = -mask_row * (rank_row - mean_t) / spread_t / every

    landed(full.at[1, theirs], in_sem.at[6])
    ga[:, 0:inner] = adapter_scale * contract((full[1] * coefficient).astype(BF16), hid[...], 1, 0)
    ga[:, inner:] = jnp.zeros((32, 4 * quarter - inner), F32)
    for r in range(nd):
        value = quarters(ga[4 * r : 4 * r + 4, :], quarter)
        gaf[r] = value
        gas[r] = value.astype(BF16)
    to_dp(lambda peer: gas.at[peer], lambda n: gar.at[n], 7)

    from_chips(0)
    run(2)
    run(3)

    landed(full.at[0, theirs], in_sem.at[5])
    p_high, p_low = high_low(full[0] * coefficient)
    right = contract(jnp.concatenate([p_high, p_low], axis=0), cot[...], 1, 0)
    gb[...] = adapter_scale * (right[0:32] + right[32:64])
    for r in range(nd):
        value = quarters(gb[4 * r : 4 * r + 4, :], quarter_b)
        gbf[r] = value
        gbs[r] = value.astype(BF16)
    to_dp(lambda peer: gbs.at[peer], lambda n: gbr.at[n], 8)

    landed(mva, lsem.at[8])
    landed(mvb, lsem.at[9])

    def own_rows(ref, quarter):
        rows = pl.ds(pl.multiple_of((i // 2) * 8, 8), 8)
        eight = ref[rows, :]
        four = jnp.where(lax.rem(i, 2) == 1, eight[4:8], eight[0:4])
        pad = 4 * quarter - four.shape[1]
        if pad:
            four = jnp.concatenate([four, jnp.zeros((4, pad), F32)], axis=1)
        return quarters(four, quarter)

    for n in range(3):
        own_a[n] = own_rows(a if n == 0 else mva.at[n - 1], quarter)
        own_b[n] = own_rows(b if n == 0 else mvb.at[n - 1], quarter_b)

    run(4)

    def adam(own, grad, received_grads):
        for n in range(nd - 1):
            grad = grad + received_grads[n].astype(F32)
        first = 0.9 * own[1] + 0.1 * grad
        second = 0.999 * own[2] + 0.001 * grad * grad
        param = own[0] - 0.004 * (first / bias_one) / (jnp.sqrt(second / bias_two) + 1e-08)
        return param, first, second

    def split(value, ref, quarter):
        columns = ref.shape[1]
        for q in range(4):
            lo, hi = q * quarter, min((q + 1) * quarter, columns)
            ref[:, lo:hi] = value[4 * q : 4 * q + 4, : hi - lo]

    for n in range(inner // 256):
        xt[256 * n : 256 * (n + 1), :] = x[:, 256 * n : 256 * (n + 1)].T
    landed(gar, in_sem.at[7])
    adam_a = adam(own_a, gaf[i], gar)
    a_send = adam_a[0].astype(BF16)
    partial = None
    for q in range(4):
        lo, hi = q * quarter, min((q + 1) * quarter, inner)
        part = contract(a_send[:, : hi - lo], xt[lo:hi, :], 1, 0)
        part = part[4 * q : 4 * q + 4]
        partial = part if partial is None else partial + part
    partial = quarters(partial, n_tok // 4)
    xa_s[...] = partial.astype(BF16)
    to_tensor(xa_s, lambda n: xa_r.at[n], 9, same_level)

    landed(gbr, in_sem.at[8])
    adam_b = adam(own_b, gbf[i], gbr)
    home = t // 2
    at_home = home == i
    split(adam_b[0].astype(BF16).astype(F32), bs, quarter_b)

    def home_copy():
        return copy_to(bs, bc.at[i], out_sem.at[1], in_sem.at[11], {"dp": home})

    @pl.when(jnp.logical_not(at_home))
    def _():
        home_copy().start()

    for value, ref in zip(adam_a, (o_pa, o_ma, o_va)):
        split(value, ref, quarter)
    for value, ref in zip(adam_b, (o_pb, o_mb, o_vb)):
        split(value, ref, quarter_b)

    run(5)

    landed(xa_r, in_sem.at[9])
    mine = partial
    for n in range(len(same_level)):
        mine = mine + xa_r[n].astype(F32)
    slot = level * nd + i
    xall[slot] = mine.astype(BF16)
    for dy, dz in PLANE:
        push(xall.at[slot], xall.at[slot], 10, plane_peer(dy, dz)).start()

    def column_copy(k):
        cols = pl.ds(128 * k, 128)
        return copy_to(
            bc.at[:, :, cols], bd, out_sem.at[2], in_sem.at[12], {"tensor": 8 * core + k}
        )

    @pl.when(at_home)
    def _():
        landed(bc.at[pl.ds(0, nd - 1)], in_sem.at[11])
        bc[i] = bs[...]
        for k in range(8):
            here = 8 * core + k == t

            @pl.when(jnp.logical_not(here))
            def _():
                column_copy(k).start()

            @pl.when(here)
            def _():
                bd[...] = bc[:, :, 128 * k : 128 * k + 128]

    keep[chips - 1] = chip_total(chips - 1) + received(4) + received(5) + received(6)

    @pl.when(2 * i + t // 8 != t)
    def _():
        landed(bd, in_sem.at[12])

    b_rows = bd[...]
    b_rows = jnp.concatenate([b_rows] * 4, axis=1).reshape(16 * nd, 128)
    row_b = lax.rem(lax.broadcasted_iota(jnp.int32, (16 * nd, 128), 0), 16) // 4
    b_parts = [jnp.where(row_b == q, b_rows, 0.0).astype(BF16) for q in range(4)]
    landed(xall.at[pl.ds(0, len(PLANE))], in_sem.at[10])
    z = xall[...].reshape(32 * nd, n_tok // 4)
    for q in range(4):
        added = contract(z, jnp.concatenate([b_parts[q], b_parts[q]], axis=0), 0, 0)
        rows = slice(q * (n_tok // 4), (q + 1) * (n_tok // 4))
        o_out[rows, :] = (keep[chips - 1, rows, :] + adapter_scale * added).astype(BF16)

    tiles = sum(pushed) // 4096
    deep = max(n for n in range(1, n_tok // 16 + 1) if tiles % n == 0)
    wide = tiles // deep
    assert sum(pushed) == tiles * 4096 and wide * 128 <= inner
    landed(x.at[pl.ds(0, 16 * deep), pl.ds(0, 128 * wide)], out_sem.at[0])

    @pl.when(jnp.logical_not(at_home))
    def _():
        home_copy().wait_send()

    @pl.when(at_home)
    def _():
        among = jnp.logical_and(t >= 8 * core, t < 8 * core + 8)

        @pl.when(among)
        def _():
            landed(bc.at[pl.ds(0, 7)], out_sem.at[2])

        @pl.when(jnp.logical_not(among))
        def _():
            landed(bc, out_sem.at[2])


def hand_over(*refs):
    *refs, sems = refs
    count = len(refs) // 2
    copies = [
        pltpu.make_async_copy(refs[n], refs[count + n], sems.at[n]) for n in range(count)
    ]
    for copy in copies:
        copy.start()
    for copy in copies:
        copy.wait()


def shards(
    hidden, cotangent, prompt_group_index, answer_token_mask, token_reward_order,
    source_lowdim_matrix, running_mean_source_matrix, running_variance_source_matrix,
    target_lowdim_matrix, running_mean_target_matrix, running_variance_target_matrix,
    frozen_down_weight, sampled_token_input,
):
    nd, nt = lax.axis_size("dp"), lax.axis_size("tensor")
    tokens, inner = hidden.shape
    width = cotangent.shape[1]
    rank = source_lowdim_matrix.shape[0]
    columns = frozen_down_weight.shape[1]
    rollout = sampled_token_input.shape[0]
    n_groups = tokens * nd // 8
    chips = nt // 2
    quarter, quarter_b = -(-inner // 512) * 128, -(-width // 512) * 128
    rows = rank // nd
    vmem, dma = pltpu.VMEM, pltpu.SemaphoreType.DMA
    scratch = [
        vmem((tokens, inner), BF16), vmem((tokens, width), BF16),
        vmem((3, 1, tokens), jnp.int32),
        vmem((rank, inner), F32), vmem((2, rank, inner), F32),
        vmem((rank, width), F32), vmem((2, rank, width), F32),
        vmem((chips, inner, 256), BF16), vmem((rollout, inner), BF16),
        vmem((inner, rollout), BF16),
        vmem((4, n_groups), F32), vmem((nd - 1, 4, n_groups), F32),
        vmem((2, 32, tokens), F32), vmem((2, 16, tokens), F32), vmem((2, 16, tokens), BF16),
        vmem((2, chips - 1, 16, tokens), BF16), vmem((2, 32, tokens), F32),
        vmem((rank, 4 * quarter), F32), vmem((nd, 16, quarter), F32), vmem((nd, 16, quarter), BF16),
        vmem((nd - 1, 16, quarter), BF16),
        vmem((rank, 4 * quarter_b), F32), vmem((nd, 16, quarter_b), F32),
        vmem((nd, 16, quarter_b), BF16), vmem((nd - 1, 16, quarter_b), BF16),
        vmem((3, 16, quarter), F32), vmem((3, 16, quarter_b), F32),
        vmem((16, rollout // 4), BF16), vmem((chips - 1, 16, rollout // 4), BF16),
        vmem((2 * nd, 16, rollout // 4), BF16), vmem((rows, width), F32), vmem((nd, rows, width), F32),
        vmem((nd, rows, 128), F32),
        vmem((chips, rollout, 128), F32), vmem((chips, rollout, 128), BF16),
        vmem((chips, rollout, 128), BF16), vmem((7, rollout, 128), BF16),
        vmem((7, rollout, 128), BF16),
        dma((10 + chips,)), dma((3,)), dma((21 + len(ARRIVALS),)),
    ]
    results = [((rollout, 128), BF16)] + [((rows, inner), F32)] * 3 + [((rows, width), F32)] * 3
    held = pl.pallas_call(
        functools.partial(kernel, nd, nt),
        out_shape=[vmem(shape, dtype) for shape, dtype in results],
        in_specs=[pl.BlockSpec(memory_space=pl.ANY)] * 13,
        out_specs=[pl.BlockSpec(memory_space=vmem)] * 7,
        scratch_shapes=scratch,
        compiler_params=pltpu.CompilerParams(
            collective_id=0, has_side_effects=True, vmem_limit_bytes=56 * 2**20
        ),
        name="grpo_step",
    )(
        hidden, cotangent,
        prompt_group_index.reshape(1, tokens), answer_token_mask.reshape(1, tokens),
        token_reward_order.reshape(1, tokens),
        source_lowdim_matrix, running_mean_source_matrix, running_variance_source_matrix,
        target_lowdim_matrix, running_mean_target_matrix, running_variance_target_matrix,
        frozen_down_weight, sampled_token_input,
    )
    held = [pltpu.with_memory_space_constraint(value, vmem) for value in held]
    return pl.pallas_call(
        hand_over,
        out_shape=tuple(jax.ShapeDtypeStruct(shape, dtype) for shape, dtype in results),
        in_specs=[pl.BlockSpec(memory_space=vmem)] * 7,
        out_specs=[pl.BlockSpec(memory_space=pl.ANY)] * 7,
        scratch_shapes=[dma((7,))],
        name="hand_over",
    )(*held)


def solution(mesh):
    factor = P(None, "tensor")
    placed = (
        P("dp", "tensor"), P("dp", "tensor"), P("dp"), P("dp"), P("dp"),
        factor, factor, factor, factor, factor, factor, P("tensor", "dp"), factor,
    )
    owned = P("dp", "tensor")
    return jax.shard_map(
        shards,
        mesh=mesh,
        in_specs=placed,
        out_specs=(P(None, ("dp", "tensor")), owned, owned, owned, owned, owned, owned),
        check_vma=False,
    )
```

```python
import functools
import math

import jax
import jax.numpy as jnp
from jax import lax
from jax.experimental import pallas as pl
from jax.experimental.pallas import tpu as pltpu
from jax.sharding import PartitionSpec as P

MESH = pl.DeviceIdType.MESH
F32 = jnp.float32
BF16 = jnp.bfloat16

adapter_scale = 2.0
bias_one = 1.0 - 0.9**10
bias_two = 1.0 - 0.999**10

BLOCKS = ((2, 1), (3, 1), (1, 1), (0, 1), (2, 0), (1, 0), (3, 0), (0, 0))
PARTS = ((0, ()), (1, (0,)), (2, ()), (4, ()), (5, (3,)), (6, ()), (3, (1, 2)))
GAPS = (1, 3, 3, 4, 6, 8)
ARRIVALS = ((0, 1), (1, 3), (3, 4), (4, 7))
SENDS = ((), (), (0,), (2,), (3, 1), (6, 4, 5))
FAR = ((2, 1), (1, 1), (3, 1), (2, 0), (0, 1), (1, 0), (3, 0))
PLANE = (
    (2, 2), (2, 1), (2, 3), (1, 2), (3, 2), (1, 1), (1, 3), (3, 1), (3, 3), (2, 0), (0, 2), (1, 0),
    (3, 0), (0, 1), (0, 3),
)


def contract(left, right, left_dim, right_dim):
    return lax.dot_general(
        left, right, (((left_dim,), (right_dim,)), ((), ())), preferred_element_type=F32
    )


def high_low(value):
    high = value.astype(BF16)
    return high, (value - high.astype(F32)).astype(BF16)


def quarters(value, width):
    return jnp.concatenate([value[:, q * width : (q + 1) * width] for q in range(4)], axis=0)


def kernel(
    nd, nt,
    hidden, cotangent, groups, mask, order, a_in, ma_in, va_in, b_in, mb_in, vb_in, weight, sampled,
    o_out, o_pa, o_ma, o_va, o_pb, o_mb, o_vb,
    hid, cot, ints, a, mva, b, mvb, w, x, xt,
    stat, stat_r, s1, cr, cs, ar, full, ga, gaf, gas, gar, gb, gbf, gbs, gbr, own_a, own_b,
    xa_s, xa_r, xall, bs, bc, bd, keep, give, got, part_s, part_r,
    lsem, out_sem, in_sem,
):
    i = lax.axis_index("dp")
    t = lax.axis_index("tensor")
    core = lax.rem(t, 2)
    place = t // 4
    level = lax.rem(t // 2, 2)
    chips = nt // 2
    inner = hid.shape[1]
    width = cot.shape[1]
    quarter = gas.shape[2]
    quarter_b = gbs.shape[2]
    n_tok = hid.shape[0]

    def tensor_peer(dx, dz, dc):
        return lax.rem(place + dx, 4) * 4 + lax.rem(level + dz, 2) * 2 + lax.rem(core + dc, 2)

    def dp_peer(dy, dz):
        return lax.rem(i // 4 + dz, 2) * 4 + lax.rem(lax.rem(i, 4) + dy, 4)

    def plane_peer(dy, dz):
        z = lax.rem((i // 4) * 2 + level + dz, 4)
        return {
            "dp": (z // 2) * 4 + lax.rem(lax.rem(i, 4) + dy, 4),
            "tensor": place * 4 + lax.rem(z, 2) * 2 + core,
        }

    same_core = [(dx, dz, 0) for dx, dz in FAR]
    tensor_all = [(dx, dz, dc) for dx, dz in FAR for dc in (1, 0)] + [(0, 0, 1)]
    same_level = [(dx, 0, dc) for dc in (1, 0) for dx in (2, 1, 3)] + [(0, 0, 1)]

    def landed(ref, sem):
        pltpu.make_async_copy(ref, ref, sem).wait()

    def load(src, dst, n):
        copy = pltpu.make_async_copy(src, dst, lsem.at[n])
        copy.start()
        return copy

    b_load = load(b_in, b, 1)
    cot_load = load(cotangent, cot, 2)

    barrier = pltpu.get_barrier_semaphore()
    for dy, dz in PLANE:
        pl.semaphore_signal(barrier, inc=1, device_id=plane_peer(dy, dz), device_id_type=MESH)
    for dx, dz, dc in tensor_all:
        pl.semaphore_signal(
            barrier, inc=1, device_id={"tensor": tensor_peer(dx, dz, dc)}, device_id_type=MESH
        )

    def w_load(s):
        dx, dz = BLOCKS[s]
        block = lax.rem(place + dx, 4) * 2 + lax.rem(level + dz, 2)
        cols = pl.ds(pl.multiple_of(block * 256, 256), 256)
        load(weight.at[:, cols], w.at[s], 10 + s)

    for n, source in enumerate((groups, mask, order)):
        load(source, ints.at[n], 0)
    a_load = load(a_in, a, 3)
    pieces = (0, 1280, 2304, inner)
    hid_load = []
    for n in range(len(pieces) - 1):
        cols = pl.ds(pieces[n], pieces[n + 1] - pieces[n])
        hid_load.append(load(hidden.at[:, cols], hid.at[:, cols], 4 + n))

    x_load = load(sampled, x, 7)
    for s in range(2):
        w_load(s)

    landed(ints, lsem.at[0])
    mask_row = ints[1].astype(F32)
    rank_row = ints[2].astype(F32)
    n_groups = stat.shape[1]
    group_id = lax.broadcasted_iota(jnp.int32, (n_groups, n_tok), 0)
    member = jnp.where(group_id == ints[0], 1.0, 0.0).astype(BF16)
    row = lax.broadcasted_iota(jnp.int32, (8, n_tok), 0)
    weighted = mask_row * rank_row
    terms = jnp.where(
        row == 0, mask_row, jnp.where(row == 1, weighted, jnp.where(row == 2, weighted * rank_row, 0.0))
    )
    stat[...] = contract(terms.astype(BF16), member, 1, 1)[0:4]

    b_load.wait()
    b_high, b_low = high_low(b[...])
    cot_load.wait()
    raw = contract(jnp.concatenate([b_high, b_low], axis=0), cot[...], 1, 1)
    s1[1] = raw[0:32] + raw[32:64]

    def copy_to(src, dst, send, recv, peer):
        return pltpu.make_async_remote_copy(
            src_ref=src, dst_ref=dst, send_sem=send, recv_sem=recv, device_id=peer, device_id_type=MESH
        )

    pushed = []

    def push(src, dst, n, peer, times=1):
        pushed.append(times * math.prod(src.shape) * jnp.dtype(src.dtype).itemsize)
        return copy_to(src, dst, out_sem.at[0], in_sem.at[n], peer)

    def to_dp(src, dst, n):
        for m, (dy, dz) in enumerate(FAR):
            peer = dp_peer(dy, dz)
            push(src(peer), dst(m), n, {"dp": peer}).start()

    def to_tensor(src, dst, n, peers):
        for m, (dx, dz, dc) in enumerate(peers):
            push(src, dst(m), n, {"tensor": tensor_peer(dx, dz, dc)}).start()

    other = {"tensor": tensor_peer(0, 0, 1)}
    theirs = pl.ds(pl.multiple_of(16 - 16 * core, 16), 16)
    ours = pl.ds(pl.multiple_of(16 * core, 16), 16)

    def to_chips(n):
        landed(cr.at[n], in_sem.at[3 + n])
        chip_sum = s1[n, ours, :] + cr[n]
        s1[n, ours, :] = chip_sum
        cs[n] = chip_sum.astype(BF16)
        to_tensor(cs.at[n], lambda m: ar.at[n, m], 1 + n, same_core)

    def from_chips(n):
        landed(ar.at[n], in_sem.at[1 + n])
        mine = s1[n, ours, :]
        for m in range(len(same_core)):
            mine = mine + ar[n, m].astype(F32)
        full[n, ours, :] = mine
        push(full.at[n, ours], full.at[n, ours], 5 + n, other).start()

    pl.semaphore_wait(barrier, len(tensor_all) + len(PLANE))
    push(s1.at[1, theirs], cr.at[1], 4, other).start()
    to_dp(lambda peer: stat, lambda n: stat_r.at[n], 0)
    to_chips(1)

    a_load.wait()
    a_half = a[...].astype(BF16)
    total = None
    for n, copy in enumerate(hid_load):
        copy.wait()
        cols = slice(pieces[n], pieces[n + 1])
        part = contract(a_half[:, cols], hid[:, cols], 1, 1)
        total = part if total is None else total + part
    s1[0] = total
    push(s1.at[0, theirs], cr.at[0], 3, other).start()
    for s in range(2, 4):
        w_load(s)
    for n, (source_a, source_b) in enumerate(((ma_in, mb_in), (va_in, vb_in))):
        load(source_a, mva.at[n], 8)
        load(source_b, mvb.at[n], 9)
    for s in range(4, chips):
        w_load(s)

    taken = set()

    def compute(lo, hi):
        def body(s, carry):
            landed(w.at[s], lsem.at[10 + s])
            block = contract(x[...], w[s], 1, 0)
            first, second = block[:, :128], block[:, 128:]
            keep[s] = jnp.where(core == 0, first, second)
            give[s] = jnp.where(core == 0, second, first).astype(BF16)
            copy_to(give.at[s], got.at[s], out_sem.at[0], in_sem.at[13 + s], other).start()
            return carry

        lax.fori_loop(lo, hi, body, 0)
        pushed.append((hi - lo) * math.prod(give.shape[1:]) * 2)

    def once(key, ref, sem):
        if key not in taken:
            landed(ref, sem)
        taken.add(key)

    def chip_total(s):
        landed(got.at[s], in_sem.at[13 + s])
        return keep[s] + got[s].astype(F32)

    ahead = {"tensor": tensor_peer(1, 0, 0)}
    behind = {"tensor": tensor_peer(3, 0, 0)}
    across = {"tensor": tensor_peer(0, 1, 0)}
    routes = (behind, behind, ahead, ahead, ahead, behind, across)

    def arrival(n):
        return [lo <= n < hi for lo, hi in ARRIVALS].index(True)

    def forward(n, value):
        part_s[n] = value.astype(BF16)
        push(part_s.at[n], part_r.at[n], 21 + arrival(n), routes[n]).start()

    def received(n):
        m = arrival(n)
        lo, hi = ARRIVALS[m]
        once(("part", m), part_r.at[pl.ds(lo, hi - lo)], in_sem.at[21 + m])
        return part_r[n].astype(F32)

    def run(gap):
        first = GAPS[gap - 1] if gap else 0
        if first < GAPS[gap]:
            if first == 0:
                x_load.wait()
            compute(first, GAPS[gap])
        for n in SENDS[gap]:
            block, parts = PARTS[n]
            value = chip_total(block)
            for m in parts:
                value = value + received(m)
            forward(n, value)

    run(0)
    to_chips(0)
    run(1)

    from_chips(1)
    landed(stat_r, in_sem.at[0])
    stats = stat[...]
    for d in range(nd - 1):
        stats = stats + stat_r[d]
    counts, sums, squares = stats[0:1], stats[1:2], stats[2:3]
    safe = jnp.maximum(counts, 1.0)
    mean = sums / safe
    spread = jnp.maximum(jnp.sqrt(jnp.maximum(squares / safe - mean * mean, 0.0)), 1.0)
    every = jnp.maximum(jnp.sum(counts, axis=1, keepdims=True), 1.0)
    table = jnp.zeros((8, n_groups), F32)
    row_g = lax.broadcasted_iota(jnp.int32, (8, n_groups), 0)
    for base, value in ((0, mean), (3, spread)):
        rest = value
        for n in range(3):
            term = rest.astype(BF16).astype(F32)
            table = jnp.where(row_g == base + n, term, table)
            rest = rest - term
    looked = contract(table.astype(BF16), member, 1, 0)
    mean_t = (looked[0:1] + looked[1:2]) + looked[2:3]
    spread_t = (looked[3:4] + looked[4:5]) + looked[5:6]
    coefficient = -mask_row * (rank_row - mean_t) / spread_t / every

    landed(full.at[1, theirs], in_sem.at[6])
    ga[:, 0:inner] = adapter_scale * contract((full[1] * coefficient).astype(BF16), hid[...], 1, 0)
    ga[:, inner:] = jnp.zeros((32, 4 * quarter - inner), F32)
    for r in range(nd):
        value = quarters(ga[4 * r : 4 * r + 4, :], quarter)
        gaf[r] = value
        gas[r] = value.astype(BF16)
    to_dp(lambda peer: gas.at[peer], lambda n: gar.at[n], 7)

    from_chips(0)
    run(2)
    run(3)

    landed(full.at[0, theirs], in_sem.at[5])
    p_high, p_low = high_low(full[0] * coefficient)
    right = contract(jnp.concatenate([p_high, p_low], axis=0), cot[...], 1, 0)
    gb[...] = adapter_scale * (right[0:32] + right[32:64])
    for r in range(nd):
        value = quarters(gb[4 * r : 4 * r + 4, :], quarter_b)
        gbf[r] = value
        gbs[r] = value.astype(BF16)
    to_dp(lambda peer: gbs.at[peer], lambda n: gbr.at[n], 8)

    landed(mva, lsem.at[8])
    landed(mvb, lsem.at[9])

    def own_rows(ref, quarter):
        rows = pl.ds(pl.multiple_of((i // 2) * 8, 8), 8)
        eight = ref[rows, :]
        four = jnp.where(lax.rem(i, 2) == 1, eight[4:8], eight[0:4])
        pad = 4 * quarter - four.shape[1]
        if pad:
            four = jnp.concatenate([four, jnp.zeros((4, pad), F32)], axis=1)
        return quarters(four, quarter)

    for n in range(3):
        own_a[n] = own_rows(a if n == 0 else mva.at[n - 1], quarter)
        own_b[n] = own_rows(b if n == 0 else mvb.at[n - 1], quarter_b)

    run(4)

    def adam(own, grad, received_grads):
        for n in range(nd - 1):
            grad = grad + received_grads[n].astype(F32)
        first = 0.9 * own[1] + 0.1 * grad
        second = 0.999 * own[2] + 0.001 * grad * grad
        param = own[0] - 0.004 * (first / bias_one) / (jnp.sqrt(second / bias_two) + 1e-08)
        return param, first, second

    def split(value, ref, quarter):
        columns = ref.shape[1]
        for q in range(4):
            lo, hi = q * quarter, min((q + 1) * quarter, columns)
            ref[:, lo:hi] = value[4 * q : 4 * q + 4, : hi - lo]

    for n in range(inner // 256):
        xt[256 * n : 256 * (n + 1), :] = x[:, 256 * n : 256 * (n + 1)].T
    landed(gar, in_sem.at[7])
    adam_a = adam(own_a, gaf[i], gar)
    a_send = adam_a[0].astype(BF16)
    partial = None
    for q in range(4):
        lo, hi = q * quarter, min((q + 1) * quarter, inner)
        part = contract(a_send[:, : hi - lo], xt[lo:hi, :], 1, 0)
        part = part[4 * q : 4 * q + 4]
        partial = part if partial is None else partial + part
    partial = quarters(partial, n_tok // 4)
    xa_s[...] = partial.astype(BF16)
    to_tensor(xa_s, lambda n: xa_r.at[n], 9, same_level)

    landed(gbr, in_sem.at[8])
    adam_b = adam(own_b, gbf[i], gbr)
    home = t // 2
    at_home = home == i
    split(adam_b[0].astype(BF16).astype(F32), bs, quarter_b)

    def home_copy():
        return copy_to(bs, bc.at[i], out_sem.at[1], in_sem.at[11], {"dp": home})

    @pl.when(jnp.logical_not(at_home))
    def _():
        home_copy().start()

    run(5)

    landed(xa_r, in_sem.at[9])
    mine = partial
    for n in range(len(same_level)):
        mine = mine + xa_r[n].astype(F32)
    slot = level * nd + i
    xall[slot] = mine.astype(BF16)
    for dy, dz in PLANE:
        push(xall.at[slot], xall.at[slot], 10, plane_peer(dy, dz)).start()

    def column_copy(k):
        cols = pl.ds(128 * k, 128)
        return copy_to(
            bc.at[:, :, cols], bd, out_sem.at[2], in_sem.at[12], {"tensor": 8 * core + k}
        )

    @pl.when(at_home)
    def _():
        landed(bc.at[pl.ds(0, nd - 1)], in_sem.at[11])
        bc[i] = bs[...]
        for k in range(8):
            here = 8 * core + k == t

            @pl.when(jnp.logical_not(here))
            def _():
                column_copy(k).start()

            @pl.when(here)
            def _():
                bd[...] = bc[:, :, 128 * k : 128 * k + 128]

    for value, ref in zip(adam_a, (o_pa, o_ma, o_va)):
        split(value, ref, quarter)
    for value, ref in zip(adam_b, (o_pb, o_mb, o_vb)):
        split(value, ref, quarter_b)

    keep[chips - 1] = chip_total(chips - 1) + received(4) + received(5) + received(6)

    @pl.when(2 * i + t // 8 != t)
    def _():
        landed(bd, in_sem.at[12])

    b_rows = bd[...]
    b_rows = jnp.concatenate([b_rows] * 4, axis=1).reshape(16 * nd, 128)
    row_b = lax.rem(lax.broadcasted_iota(jnp.int32, (16 * nd, 128), 0), 16) // 4
    b_parts = [jnp.where(row_b == q, b_rows, 0.0).astype(BF16) for q in range(4)]
    landed(xall.at[pl.ds(0, len(PLANE))], in_sem.at[10])
    z = xall[...].reshape(32 * nd, n_tok // 4)
    for q in range(4):
        added = contract(z, jnp.concatenate([b_parts[q], b_parts[q]], axis=0), 0, 0)
        rows = slice(q * (n_tok // 4), (q + 1) * (n_tok // 4))
        o_out[rows, :] = (keep[chips - 1, rows, :] + adapter_scale * added).astype(BF16)

    tiles = sum(pushed) // 4096
    deep = max(n for n in range(1, n_tok // 16 + 1) if tiles % n == 0)
    wide = tiles // deep
    assert sum(pushed) == tiles * 4096 and wide * 128 <= inner
    landed(x.at[pl.ds(0, 16 * deep), pl.ds(0, 128 * wide)], out_sem.at[0])

    @pl.when(jnp.logical_not(at_home))
    def _():
        home_copy().wait_send()

    @pl.when(at_home)
    def _():
        among = jnp.logical_and(t >= 8 * core, t < 8 * core + 8)

        @pl.when(among)
        def _():
            landed(bc.at[pl.ds(0, 7)], out_sem.at[2])

        @pl.when(jnp.logical_not(among))
        def _():
            landed(bc, out_sem.at[2])


def hand_over(*refs):
    *refs, sems = refs
    count = len(refs) // 2
    copies = [
        pltpu.make_async_copy(refs[n], refs[count + n], sems.at[n]) for n in range(count)
    ]
    for copy in copies:
        copy.start()
    for copy in copies:
        copy.wait()


def shards(
    hidden, cotangent, prompt_group_index, answer_token_mask, token_reward_order,
    source_lowdim_matrix, running_mean_source_matrix, running_variance_source_matrix,
    target_lowdim_matrix, running_mean_target_matrix, running_variance_target_matrix,
    frozen_down_weight, sampled_token_input,
):
    nd, nt = lax.axis_size("dp"), lax.axis_size("tensor")
    tokens, inner = hidden.shape
    width = cotangent.shape[1]
    rank = source_lowdim_matrix.shape[0]
    columns = frozen_down_weight.shape[1]
    rollout = sampled_token_input.shape[0]
    n_groups = tokens * nd // 8
    chips = nt // 2
    quarter, quarter_b = -(-inner // 512) * 128, -(-width // 512) * 128
    rows = rank // nd
    vmem, dma = pltpu.VMEM, pltpu.SemaphoreType.DMA
    scratch = [
        vmem((tokens, inner), BF16), vmem((tokens, width), BF16),
        vmem((3, 1, tokens), jnp.int32),
        vmem((rank, inner), F32), vmem((2, rank, inner), F32),
        vmem((rank, width), F32), vmem((2, rank, width), F32),
        vmem((chips, inner, 256), BF16), vmem((rollout, inner), BF16),
        vmem((inner, rollout), BF16),
        vmem((4, n_groups), F32), vmem((nd - 1, 4, n_groups), F32),
        vmem((2, 32, tokens), F32), vmem((2, 16, tokens), F32), vmem((2, 16, tokens), BF16),
        vmem((2, chips - 1, 16, tokens), BF16), vmem((2, 32, tokens), F32),
        vmem((rank, 4 * quarter), F32), vmem((nd, 16, quarter), F32), vmem((nd, 16, quarter), BF16),
        vmem((nd - 1, 16, quarter), BF16),
        vmem((rank, 4 * quarter_b), F32), vmem((nd, 16, quarter_b), F32),
        vmem((nd, 16, quarter_b), BF16), vmem((nd - 1, 16, quarter_b), BF16),
        vmem((3, 16, quarter), F32), vmem((3, 16, quarter_b), F32),
        vmem((16, rollout // 4), BF16), vmem((chips - 1, 16, rollout // 4), BF16),
        vmem((2 * nd, 16, rollout // 4), BF16), vmem((rows, width), F32), vmem((nd, rows, width), F32),
        vmem((nd, rows, 128), F32),
        vmem((chips, rollout, 128), F32), vmem((chips, rollout, 128), BF16),
        vmem((chips, rollout, 128), BF16), vmem((7, rollout, 128), BF16),
        vmem((7, rollout, 128), BF16),
        dma((10 + chips,)), dma((3,)), dma((21 + len(ARRIVALS),)),
    ]
    results = [((rollout, 128), BF16)] + [((rows, inner), F32)] * 3 + [((rows, width), F32)] * 3
    held = pl.pallas_call(
        functools.partial(kernel, nd, nt),
        out_shape=[vmem(shape, dtype) for shape, dtype in results],
        in_specs=[pl.BlockSpec(memory_space=pl.ANY)] * 13,
        out_specs=[pl.BlockSpec(memory_space=vmem)] * 7,
        scratch_shapes=scratch,
        compiler_params=pltpu.CompilerParams(
            collective_id=0, has_side_effects=True, vmem_limit_bytes=56 * 2**20
        ),
        name="grpo_step",
    )(
        hidden, cotangent,
        prompt_group_index.reshape(1, tokens), answer_token_mask.reshape(1, tokens),
        token_reward_order.reshape(1, tokens),
        source_lowdim_matrix, running_mean_source_matrix, running_variance_source_matrix,
        target_lowdim_matrix, running_mean_target_matrix, running_variance_target_matrix,
        frozen_down_weight, sampled_token_input,
    )
    held = [pltpu.with_memory_space_constraint(value, vmem) for value in held]
    return pl.pallas_call(
        hand_over,
        out_shape=tuple(jax.ShapeDtypeStruct(shape, dtype) for shape, dtype in results),
        in_specs=[pl.BlockSpec(memory_space=vmem)] * 7,
        out_specs=[pl.BlockSpec(memory_space=pl.ANY)] * 7,
        scratch_shapes=[dma((7,))],
        name="hand_over",
    )(*held)


def solution(mesh):
    factor = P(None, "tensor")
    placed = (
        P("dp", "tensor"), P("dp", "tensor"), P("dp"), P("dp"), P("dp"),
        factor, factor, factor, factor, factor, factor, P("tensor", "dp"), factor,
    )
    owned = P("dp", "tensor")
    return jax.shard_map(
        shards,
        mesh=mesh,
        in_specs=placed,
        out_specs=(P(None, ("dp", "tensor")), owned, owned, owned, owned, owned, owned),
        check_vma=False,
    )
```
